256 devices in a mesh: gx: 8 (over z), gy: 4 (over y), gz: 8 (over x, core).
Axes of the slice: x: 4, y: 4, z: 8, core: 2. Of those that a mesh axis runs over, the one named last changes fastest.
Arguments:
- offsets: float32 [3, 1048576], P(None, ('gx', 'gy', 'gz')), may hold values from 0 to 1
- strength: float32 [3, 1048576], P(None, ('gx', 'gy', 'gz')), may hold values from -0.012 to 0.012
- ghost_list: int32 [393216], P(('gx', 'gy', 'gz')), may hold values from 0 to 4095
- pair_targets: int32 [32768], P(('gx', 'gy', 'gz')), may hold values from 0 to 31
- pair_sources: int32 [32768], P(('gx', 'gy', 'gz')), may hold values from 0 to 103
- owners: int32 [8192, 1], P(('gx', 'gy', 'gz')), may hold values from 0 to 31; in each aligned block of 32 rows (0 to 31, 32 to 63, ...) at most 2 rows name the same one
Outputs:
- moved_positions: float32 [16384, 3, 128], P(('gx', 'gy', 'gz'))
- moved_velocity: float32 [16384, 3, 128], P(('gx', 'gy', 'gz'))
The draws below stay inside these ranges and needn't reach their ends.
Inputs may be any that keep to these rules, and one draw needn't show every extreme that they name: `owners`: among the 32 blocks of one domain no owner is named more than 2 times.
All inputs are finite; a program needn't handle non-finite values.
Results may differ from the reference program's by a relative error of at most 0.0003.
Values sent between devices are 32-bit elements; how exact they have to be, the bound alone decides.
A program may use at most 128 MiB of HBM per device.

```python
import math
import jax
import jax.numpy as jnp
import numpy as np
from jax import lax

SEG = 4096
ORDER = 5
GHOST = 1536
NPAIR = 128
CAP = 2
NSEG = 1048576
N_GX = 8
N_GY = 4
N_GZ = 8
DEVICES = 256


def touch_ends(result, rng, low, high):
    spot = [jax.random.randint(jax.random.fold_in(rng, axis), (), 0, length) for axis, length in enumerate(result.shape)]
    widest = result.shape.index(max(result.shape))
    next_to = spot[:widest] + [(spot[widest] + 1) % result.shape[widest]] + spot[widest + 1:]
    return result.at[tuple(spot)].set(low).at[tuple(next_to)].set(high)


def steps_of(stream_key, extent, split, low, largest):
    loudness, own = 1.0, jax.random.fold_in(stream_key, 6)
    for axis_at, parts in split:
        steps = jnp.exp(jax.random.uniform(jax.random.fold_in(own, axis_at), (parts,), jnp.float32, low / len(split), largest / len(split)))
        loudness = loudness * jnp.repeat(steps, extent[axis_at] // parts).reshape([-1 if axis == axis_at else 1 for axis in range(len(extent))])
    return loudness


def shared_out(stream_key, own, number, rows, amount, top, reach, lean):
    ranking = jax.random.permutation(stream_key, amount)
    crowded, common = shares(amount, rows * top, reach, lean, True), shares(amount, rows * top, reach, lean, False)
    places = jnp.arange(amount)

    def named(tallies, offset_by):
        used = int((tallies > 0).sum())
        fixed = max(1, used // 4)
        moved = fixed + (places - fixed + offset_by * (used - fixed)) % max(1, amount - fixed)
        return jnp.zeros((amount,), jnp.int32).at[ranking[jnp.where(places < fixed, places, moved)]].set(jnp.asarray(tallies, jnp.int32))

    tallies = jnp.where(number % 4 == 0, named(crowded, number // 4), named(common, number - number // 4 - 1))
    mixed = jax.random.permutation(jax.random.fold_in(own, 3), amount)
    donor, receiver = mixed[0:amount // 2 * 2:2], mixed[1:amount // 2 * 2:2]
    slack = jnp.minimum(tallies[donor] - 1, reach - tallies[receiver]) // 2
    slack = jnp.where((donor == ranking[0]) | (receiver == ranking[0]) | (tallies[receiver] == 0), 0, jnp.maximum(slack, 0))
    moved = jax.random.randint(jax.random.fold_in(own, 4), (amount // 2,), 0, 1 << 20) % (slack + 1)
    tallies = tallies.at[donor].add(-moved).at[receiver].add(moved)
    labels = jnp.searchsorted(jnp.cumsum(tallies), jnp.arange(rows * top), side="right").astype(jnp.int32)
    grid = labels.reshape(top, rows).T
    grid = grid[jax.random.permutation(jax.random.fold_in(own, 1), rows)]
    offset_by = jax.random.randint(jax.random.fold_in(own, 2), (rows, 1), 0, top)
    return jnp.take_along_axis(grid, (jnp.arange(top)[None, :] + offset_by) % top, axis=1)


def shares(number_of, total, most, slope, full):
    portions = [(1 << 20) // math.isqrt(standing ** slope) + 1 for standing in range(1, number_of + 1)]
    largest = most if full else min(most, max(-(-total // number_of), total * portions[0] // sum(portions)))
    least = 1 if total - largest >= number_of - 1 else 0
    holding, rest = [largest] + [least] * (number_of - 1), total - largest - least * (number_of - 1)
    while rest > 0:
        free = [i for i in range(1, number_of) if holding[i] < largest] or [i for i in range(1, number_of) if holding[i] < most]
        mass, budget = sum([portions[i] for i in free]), rest
        for i in free:
            more = min(most - holding[i], max(1, budget * portions[i] // mass), rest)
            holding[i] = holding[i] + more
            rest = rest - more
    return np.array(holding)


def gaussian(key, shape, width, limit, cuts=(), kind=jnp.bfloat16):
    loudness = steps_of(key, shape, cuts, -0.22, 0.18) if cuts else 1.0
    values = jax.random.normal(key, shape, jnp.float32) * width * loudness
    return jnp.minimum(jnp.maximum(values, -limit), limit).astype(kind)


def setup_inputs(seed: int = 0) -> dict:
    arg_keys = jax.random.split(jax.random.key(seed), 7)
    offsets = jnp.clip(1.0 * jax.random.uniform(arg_keys[0], (3, NSEG), jnp.float32) ** steps_of(arg_keys[0], (3, NSEG), ((1, 256),), -0.2, 0.2), 0.0, 1.0)
    strength = gaussian(arg_keys[1], (3, NSEG), 0.002, 0.012, ((1, 256),), jnp.float32)
    ghost_list = touch_ends(jax.random.randint(arg_keys[2], (DEVICES * GHOST,), 0, SEG), jax.random.fold_in(arg_keys[2], 1), 0, SEG - 1).astype(jnp.int32)
    pair_targets = touch_ends(jax.random.randint(arg_keys[3], (DEVICES * NPAIR,), 0, SEG // 128), jax.random.fold_in(arg_keys[3], 1), 0, (SEG // 128) - 1).astype(jnp.int32)
    pair_sources = touch_ends(jax.random.randint(arg_keys[4], (DEVICES * NPAIR,), 0, SEG // 128 + 6 * (GHOST // 128)), jax.random.fold_in(arg_keys[4], 1), 0, (SEG // 128 + 6 * (GHOST // 128)) - 1).astype(jnp.int32)
    owners_keys = jax.random.split(jax.random.fold_in(arg_keys[5], 1), (DEVICES * SEG // 128) // (SEG // 128))
    owners_turns = jax.random.permutation(jax.random.fold_in(arg_keys[5], 3), (DEVICES * SEG // 128) // (SEG // 128))
    owners = jax.vmap(lambda own, number: shared_out(jax.random.fold_in(arg_keys[5], 2), own, number, SEG // 128, N_GX * N_GY, 1, CAP, 2))(owners_keys, owners_turns).reshape((DEVICES * SEG // 128, 1))
    return {"offsets": offsets, "strength": strength, "ghost_list": ghost_list, "pair_targets": pair_targets, "pair_sources": pair_sources, "owners": owners}


core_sq = 0.0025
time_step = 0.1
highest = lax.Precision.HIGHEST

def exponent_table():
    entries = []
    for degree in range(ORDER + 1):
        for leading in range(degree, -1, -1):
            for middle in range(degree - leading, -1, -1):
                entries.append((leading, middle, degree - leading - middle))
    return np.array(entries, dtype=np.int32)

def factorial_table():
    return np.array([float(np.prod([math.factorial(int(exponent)) for exponent in triple])) for triple in exponent_table()], dtype=np.float32)

def monomials(relative):
    powers = exponent_table()
    stacks = [jnp.stack([relative[axis_id] ** degree for degree in range(ORDER + 1)]) for axis_id in range(3)]
    return stacks[0][powers[:, 0]] * stacks[1][powers[:, 1]] * stacks[2][powers[:, 2]]

def derivative_tables():
    powers = exponent_table()
    factors = factorial_table()
    starts = np.cumsum([0] + [3 ** degree for degree in range(ORDER + 1)])
    entry_count = powers.shape[0]
    index_table = np.zeros((entry_count, entry_count), dtype=np.int32)
    weight_table = np.zeros((entry_count, entry_count), dtype=np.float32)
    for outer_pos in range(entry_count):
        for inner_pos in range(entry_count):
            merged = powers[outer_pos] + powers[inner_pos]
            degree = int(np.sum(merged))
            if degree <= ORDER:
                flat_pos = 0
                for axis_id in range(3):
                    for repeat in range(int(merged[axis_id])):
                        flat_pos = flat_pos * 3 + axis_id
                index_table[outer_pos, inner_pos] = starts[degree] + flat_pos
                weight_table[outer_pos, inner_pos] = (-1.0) ** int(np.sum(powers[inner_pos])) / float(factors[inner_pos])
    return (index_table, weight_table)

def potential(separation):
    return lax.rsqrt(jnp.sum(separation * separation) + core_sq)

def jacobian_of(function):

    def derived(separation):
        value, pullback = jax.vjp(function, separation)
        count = value.size
        basis = jnp.eye(count, dtype=value.dtype).reshape((count,) + value.shape)
        rows = jax.vmap(pullback)(basis)[0]
        return rows.reshape(value.shape + separation.shape)
    return derived

def kernel_derivatives(separation):
    pieces = []
    current = potential
    for degree in range(ORDER + 1):
        pieces.append(jnp.ravel(current(separation)))
        current = jacobian_of(current)
    return jnp.concatenate(pieces)

def local_expansion(separations, moments, weights):
    index_table, weight_table = derivative_tables()
    derivs = jax.vmap(kernel_derivatives)(separations)
    operator = derivs[:, index_table] * jnp.asarray(weight_table, jnp.float32)[None] * weights[:, None, None]
    return jnp.einsum('sba,sac->bc', operator, moments, precision=highest)

def far_field(relative, expansion):
    scaled = monomials(relative) / jnp.asarray(factorial_table(), jnp.float32)[:, None]
    return jnp.dot(expansion.T, scaled, precision=highest)

def moments_about(positions, strength, centre):
    return jnp.dot(monomials(positions - centre[:, None]), strength.T, precision=highest)

def far_sources(slab_centre, index_x, index_y, tall, column_moments):
    column_ids = jnp.arange(column_moments.shape[0], dtype=jnp.int32)
    column_x = column_ids // tall
    column_y = column_ids % tall
    column_centres = jnp.stack([column_x.astype(jnp.float32) + 0.5, column_y.astype(jnp.float32) + 0.5, jnp.full(column_ids.shape, 0.5, jnp.float32)], axis=1)
    column_weights = (jnp.maximum(jnp.abs(column_x - index_x), jnp.abs(column_y - index_y)) >= 3).astype(jnp.float32)
    separations = slab_centre[None, :] - column_centres
    return local_expansion(separations, column_moments, column_weights)

def near_field(positions, strength, ghosts, targets, sources):
    tile_count = positions.shape[1] // 128
    ghost_tiles = ghosts.shape[2] // 128
    own_pos = positions.reshape(3, tile_count, 128).transpose(1, 0, 2)
    own_str = strength.reshape(3, tile_count, 128).transpose(1, 0, 2)
    ghost_pos = ghosts[:, :3].reshape(6, 3, ghost_tiles, 128).transpose(0, 2, 1, 3).reshape(6 * ghost_tiles, 3, 128)
    ghost_str = ghosts[:, 3:].reshape(6, 3, ghost_tiles, 128).transpose(0, 2, 1, 3).reshape(6 * ghost_tiles, 3, 128)
    source_pos = jnp.concatenate([own_pos, ghost_pos])
    source_str = jnp.concatenate([own_str, ghost_str])
    pair_count = targets.shape[0]
    block_size = 64 if pair_count % 64 == 0 else pair_count
    target_blocks = targets.reshape(pair_count // block_size, block_size)
    source_blocks = sources.reshape(pair_count // block_size, block_size)
    tile_ids = jnp.arange(tile_count, dtype=jnp.int32)

    def accumulate(totals, pair_block):
        target_ids, source_ids = pair_block
        here = own_pos[target_ids]
        there = source_pos[source_ids]
        pushed = source_str[source_ids]
        gap = here[:, 0, :, None] - there[:, 0, None, :]
        dist_sq = gap * gap
        for axis_id in range(1, 3):
            gap = here[:, axis_id, :, None] - there[:, axis_id, None, :]
            dist_sq = dist_sq + gap * gap
        kernel_block = lax.rsqrt(dist_sq + core_sq)
        contrib = jnp.einsum('bij,bkj->bki', kernel_block, pushed, precision=highest)
        selector = (tile_ids[:, None] == target_ids[None, :]).astype(jnp.float32)
        return (totals + jnp.einsum('tb,bki->tki', selector, contrib, precision=highest), None)
    totals, unused = lax.scan(accumulate, jnp.zeros((tile_count, 3, 128), jnp.float32), (target_blocks, source_blocks))
    return totals.transpose(1, 0, 2).reshape(3, tile_count * 128)

def place_blocks(fields, owner_ids, group, capacity):
    block_count = owner_ids.shape[0]
    block_ids = jnp.arange(block_count, dtype=jnp.int32)
    earlier = (owner_ids[None, :] == owner_ids[:, None]) & (block_ids[None, :] < block_ids[:, None])
    slot_ids = owner_ids * capacity + lax.optimization_barrier(jnp.sum(earlier.astype(jnp.int32), axis=1))
    placer = (slot_ids[:, None] == jnp.arange(group * capacity, dtype=jnp.int32)[None, :]).astype(jnp.float32)
    tiles = fields.reshape(6, block_count, 128).transpose(1, 0, 2).reshape(block_count, 768)
    return jnp.dot(placer.T, tiles, precision=highest).reshape(group, capacity, 6, 128)

def from_lower(field, axis_id):
    length = field.shape[axis_id]
    kept = lax.slice_in_dim(field, 0, length - 1, axis=axis_id)
    return jnp.concatenate([jnp.zeros_like(lax.slice_in_dim(field, 0, 1, axis=axis_id)), kept], axis=axis_id)

def from_upper(field, axis_id):
    length = field.shape[axis_id]
    kept = lax.slice_in_dim(field, 1, length, axis=axis_id)
    return jnp.concatenate([kept, jnp.zeros_like(lax.slice_in_dim(field, 0, 1, axis=axis_id))], axis=axis_id)

def reference(offsets, strength, ghost_list, pair_targets, pair_sources, owners):
    group = N_GX * N_GY
    device_ids = jnp.arange(DEVICES, dtype=jnp.int32)
    index_x = device_ids // (N_GY * N_GZ)
    index_y = device_ids // N_GZ % N_GY
    index_z = device_ids % N_GZ
    side_z = 1.0 / N_GZ
    corners = jnp.stack([index_x.astype(jnp.float32), index_y.astype(jnp.float32), index_z.astype(jnp.float32) * side_z], axis=1)
    sides = jnp.asarray([1.0, 1.0, side_z], jnp.float32)
    positions = corners[:, :, None] + offsets.reshape(3, DEVICES, SEG).transpose(1, 0, 2) * sides[None, :, None]
    strength_dev = strength.reshape(3, DEVICES, SEG).transpose(1, 0, 2)
    slab_centres = corners + 0.5 * sides[None, :]
    column_centres = jnp.stack([index_x.astype(jnp.float32) + 0.5, index_y.astype(jnp.float32) + 0.5, jnp.full((DEVICES,), 0.5, jnp.float32)], axis=1)
    ghost_ids = ghost_list.reshape(DEVICES, GHOST)
    target_ids = pair_targets.reshape(DEVICES, NPAIR)
    source_ids = pair_sources.reshape(DEVICES, NPAIR)

    def leaf_moments(items):
        return moments_about(items[0], items[1], items[2])
    velocity = jnp.zeros_like(positions)
    for step_number in range(2):
        column_parts = lax.map(leaf_moments, (positions, strength_dev, column_centres))
        column_moments = lax.optimization_barrier(jnp.sum(column_parts.reshape(group, N_GZ, -1, 3), axis=1))
        packed = jnp.concatenate([positions, strength_dev], axis=1)
        chosen = jnp.take_along_axis(packed, ghost_ids[:, None, :], axis=2).reshape(N_GX, N_GY, N_GZ, 6, GHOST)
        neighbours = jnp.stack([from_lower(chosen, 0), from_upper(chosen, 0), from_lower(chosen, 1), from_upper(chosen, 1), from_lower(chosen, 2), from_upper(chosen, 2)], axis=3).reshape(DEVICES, 6, 6, GHOST)

        def device_forces(items):
            pos_here, str_here, ghost_here, target_here, source_here, device_id = items
            slab_centre = slab_centres[device_id]
            expansion = far_sources(slab_centre, index_x[device_id], index_y[device_id], N_GY, column_moments)
            near = near_field(pos_here, str_here, ghost_here, target_here, source_here)
            return near + far_field(pos_here - slab_centre[:, None], expansion)
        velocity = lax.map(device_forces, (positions, strength_dev, neighbours, target_ids, source_ids, device_ids))
        positions = positions + time_step * velocity
    data = jnp.concatenate([positions, velocity], axis=1)
    owner_rows = owners[:, 0].reshape(DEVICES, SEG // 128)

    def place_one(items):
        return place_blocks(items[0], items[1], group, CAP)
    sent = lax.map(place_one, (data, owner_rows))
    received = sent.reshape(N_GX, N_GY, N_GZ, N_GX, N_GY, CAP, 6, 128).transpose(3, 4, 2, 0, 1, 5, 6, 7).reshape(DEVICES * group * CAP, 6, 128)
    return (received[:, :3], received[:, 3:])
```

```python
import functools
import math

import jax
import jax.numpy as jnp
import numpy as np
from jax import lax
from jax.experimental import pallas as pl
from jax.experimental.pallas import tpu as pltpu
from jax.sharding import PartitionSpec as P

SEG = 4096
ORDER = 5
GHOST = 1536
NPAIR = 128
CAP = 2
LANES = 128
TILES = SEG // LANES
GHOST_TILES = GHOST // LANES
SOURCES = TILES + 6 * GHOST_TILES
UNROLL = 16

core_sq = 0.0025
time_step = 0.1
bf16 = jnp.bfloat16
f32 = jnp.float32
MESH = pl.DeviceIdType.MESH

TRIPLES = [
    (i, j, d - i - j)
    for d in range(ORDER + 1)
    for i in range(d, -1, -1)
    for j in range(d - i, -1, -1)
]
PLACE = {triple: at for at, triple in enumerate(TRIPLES)}
COUNT = len(TRIPLES)
MESSAGE = 256


def factorial(triple):
    return float(math.prod(math.factorial(e) for e in triple))


def lowered(triple, axis, by=1):
    out = list(triple)
    out[axis] -= by
    return tuple(out)


def monomials(coords):
    made = {}
    for triple in TRIPLES:
        if sum(triple) == 0:
            made[triple] = None
        else:
            axis = next(a for a in range(3) if triple[a])
            below = made[lowered(triple, axis)]
            made[triple] = coords[axis] if below is None else below * coords[axis]
    return made


def derivatives(separation):
    rx, ry, rz = separation
    inverse = 1.0 / (rx * rx + ry * ry + rz * rz + core_sq)
    taylor = {(0, 0, 0): lax.sqrt(inverse)}
    for triple in TRIPLES[1:]:
        n = sum(triple)
        first, second = None, None
        for axis in range(3):
            if triple[axis] >= 1:
                term = separation[axis] * taylor[lowered(triple, axis)]
                first = term if first is None else first + term
            if triple[axis] >= 2:
                term = taylor[lowered(triple, axis, 2)]
                second = term if second is None else second + term
        total = first * (-(2.0 * n - 1.0) / n)
        if second is not None:
            total = total - second * ((n - 1.0) / n)
        taylor[triple] = total * inverse
    return {t: v if factorial(t) == 1.0 else v * factorial(t) for t, v in taylor.items()}


def split3(value):
    high = value.astype(bf16).astype(f32)
    rest = value - high
    middle = rest.astype(bf16).astype(f32)
    return high, middle, rest - middle


def halves(value):
    high = value.astype(bf16)
    return high, (value - high.astype(f32)).astype(bf16)


def kernel(
    sizes,
    offsets, strength, ghost_list, targets, target_row, sources, owners,
    out_pos, out_vel,
    own, ghost_out, ghost_in, target_feat, source_feat, source_str, contrib, partial,
    message, column_in, plane_in, gathered, turned, local, far_weights, block_out, block_in,
    ghost_send, ghost_recv, column_send, column_recv, plane_send, plane_recv, block_send, block_recv,
):
    wide, tall, deep = sizes
    plane = wide * tall
    gx, gy, gz = lax.axis_index("gx"), lax.axis_index("gy"), lax.axis_index("gz")
    rank = gx * tall + gy
    side = 1.0 / deep
    sub = lax.broadcasted_iota(jnp.int32, (8, LANES), 0)

    def along(d):
        return (gx, gy, lax.rem(gz + d, deep))

    def across(d):
        other = lax.rem(rank + d, plane)
        return (other // tall, lax.rem(other, tall), gz)

    barrier = pltpu.get_barrier_semaphore()

    def greet_column(d, c):
        pl.semaphore_signal(barrier, inc=1, device_id=along(d), device_id_type=MESH)
        return c

    def greet_plane(d, c):
        pl.semaphore_signal(barrier, inc=1, device_id=across(d), device_id_type=MESH)
        return c

    lax.fori_loop(1, deep, greet_column, 0)
    lax.fori_loop(1, plane, greet_plane, 0)

    position = (gx, gy, gz)
    slots = []
    for axis, count in enumerate((wide, tall, deep)):
        at = position[axis]
        up = tuple(p + 1 if i == axis else p for i, p in enumerate(position))
        down = tuple(p - 1 if i == axis else p for i, p in enumerate(position))
        step = side if axis == 2 else 1.0
        slots.append((axis, -step, at > 0, at < count - 1, up))
        slots.append((axis, step, at < count - 1, at > 0, down))

    scale = jnp.where(lax.broadcasted_iota(jnp.int32, (3, LANES), 0) == 2, side, 1.0)
    own[...] = jnp.zeros_like(own)
    for t in range(TILES):
        lanes = slice(t * LANES, (t + 1) * LANES)
        own[8 * t : 8 * t + 3, :] = (offsets[:, lanes] - 0.5) * scale
        own[8 * t + 3 : 8 * t + 6, :] = strength[:, lanes]

    def dense(row):
        return own[pl.ds(row, TILES, stride=8), :]

    dense_strength = [dense(3 + k) for k in range(3)]

    lane = lax.broadcasted_iota(jnp.int32, (4, plane), 1)
    shift = tall.bit_length() - 1
    source_x, source_y = lane >> shift, lane & (tall - 1)
    away_x, away_y = gx - source_x, gy - source_y
    is_far = jnp.maximum(jnp.abs(away_x), jnp.abs(away_y)) >= 3

    column = owners[...]
    rows_i = lax.broadcasted_iota(jnp.int32, (TILES, TILES), 0)
    cols_i = lax.broadcasted_iota(jnp.int32, (TILES, TILES), 1)
    column_f = jnp.broadcast_to(column.astype(f32), (TILES, TILES))
    row_f = jnp.sum(jnp.where(rows_i == cols_i, column_f, 0.0), axis=0, keepdims=True)
    earlier = jnp.where((column_f == row_f) & (rows_i < cols_i), 1.0, 0.0)
    slot_f = jnp.sum(earlier, axis=0, keepdims=True) * plane + row_f
    slot_rows = lax.broadcasted_iota(jnp.int32, (CAP * plane, TILES), 0).astype(f32)
    placer = jnp.where(slot_rows == slot_f, 1.0, 0.0).astype(bf16)
    placer = jnp.concatenate([placer, placer, placer], axis=1)

    def place(which, k, field):
        parts = jnp.concatenate([p.astype(bf16) for p in split3(field)], axis=0)
        placed = jnp.dot(placer, parts, preferred_element_type=f32)
        for r in range(CAP):
            rows = pl.ds(which * plane * 8 + 3 * r + k, plane, stride=8)
            block_out[rows, :] = placed[r * plane : (r + 1) * plane]

    def block_rows(which, o):
        return pl.ds(pl.multiple_of(which * plane * 8 + 8 * o, 8), 8)

    def block_copy(which, d):
        target = across(d)
        other = target[0] * tall + target[1]
        return pltpu.make_async_remote_copy(
            src_ref=block_out.at[block_rows(which, other)],
            dst_ref=block_in.at[block_rows(which, rank)],
            send_sem=block_send.at[which],
            recv_sem=block_recv.at[which],
            device_id=target,
            device_id_type=MESH,
        )

    def send_blocks(which):
        def send(d, c):
            block_copy(which, d).start()
            return c

        lax.fori_loop(1, plane, send, 0)
        block_in[block_rows(which, rank), :] = block_out[block_rows(which, rank), :]

    def all_blocks(which):
        rows = pl.ds(which * plane * 8, (plane - 1) * 8)
        return pltpu.make_async_remote_copy(
            src_ref=block_out.at[rows],
            dst_ref=block_in.at[rows],
            send_sem=block_send.at[which],
            recv_sem=block_recv.at[which],
            device_id=across(1),
            device_id_type=MESH,
        )

    def ghost_copy(step, j):
        return pltpu.make_async_remote_copy(
            src_ref=ghost_out.at[step],
            dst_ref=ghost_in.at[step, j],
            send_sem=ghost_send.at[step, j],
            recv_sem=ghost_recv.at[step, j],
            device_id=slots[j][4],
            device_id_type=MESH,
        )

    def column_copy(step, d):
        return pltpu.make_async_remote_copy(
            src_ref=message.at[step, 0],
            dst_ref=column_in.at[step, d - 1],
            send_sem=column_send.at[step],
            recv_sem=column_recv.at[step],
            device_id=along(d),
            device_id_type=MESH,
        )

    def all_column(step):
        return pltpu.make_async_remote_copy(
            src_ref=column_in.at[step],
            dst_ref=column_in.at[step],
            send_sem=column_send.at[step],
            recv_sem=column_recv.at[step],
            device_id=along(1),
            device_id_type=MESH,
        )

    def plane_copy(step, d):
        return pltpu.make_async_remote_copy(
            src_ref=message.at[step, 1],
            dst_ref=plane_in.at[step, rank],
            send_sem=plane_send.at[step],
            recv_sem=plane_recv.at[step],
            device_id=across(d),
            device_id_type=MESH,
        )

    def all_plane(step):
        rows = plane_in.at[step, pl.ds(0, plane - 1)]
        return pltpu.make_async_remote_copy(
            src_ref=rows,
            dst_ref=rows,
            send_sem=plane_send.at[step],
            recv_sem=plane_recv.at[step],
            device_id=across(1),
            device_id_type=MESH,
        )

    for step in range(2):
        for j in range(6):

            @pl.when(jnp.logical_not(slots[j][2]))
            def _():
                ghost_in[step, j] = jnp.zeros((GHOST_TILES, 8, LANES), f32)

    zeros8 = jnp.zeros((8, LANES), f32)

    def squares(raw):
        return jnp.sum(jnp.where(sub < 3, raw * raw, 0.0), axis=0, keepdims=True)

    def source_rows(raw):
        mixed = jnp.where(sub < 3, raw, jnp.where(sub < 6, pltpu.roll(raw, 3, 0), 1.0))
        value = jnp.where(sub == 6, squares(raw), mixed)
        high, middle, low = split3(value)
        return [
            high,
            jnp.where(sub == 7, high, middle),
            jnp.where((sub < 3) | (sub == 6), low, high),
            zeros8,
        ]

    def target_rows(raw):
        mixed = jnp.where(sub < 3, -2.0 * raw, jnp.where(sub < 6, -2.0 * pltpu.roll(raw, 3, 0), 1.0))
        value = jnp.where(sub == 7, squares(raw) + core_sq, mixed)
        high, middle, low = split3(value)
        second = (sub >= 3) & (sub < 6)
        last = second | (sub == 7)
        return [
            jnp.where(second, middle, high),
            jnp.where(last, middle, high),
            jnp.where(last, low, high),
            zeros8,
        ]

    def strength_rows(raw):
        high = raw.astype(bf16).astype(f32)
        return jnp.concatenate([high, raw - high], axis=0).astype(bf16)

    def source_quad(quad, tiles):
        rows = [row for raw in tiles for row in source_rows(raw)]
        source_feat[quad] = jnp.transpose(jnp.concatenate(rows, axis=0)).astype(bf16)

    target_feat[...] = jnp.zeros_like(target_feat)

    chosen = (lax.broadcasted_iota(jnp.int32, (TILES, NPAIR), 0) == target_row[...].reshape(1, NPAIR))
    chosen = jnp.where(chosen, 1.0, 0.0).astype(bf16)
    chosen = jnp.concatenate([chosen, chosen], axis=1)

    pl.semaphore_wait(barrier, deep - 1 + plane - 1)

    velocity = None
    for step in range(2):

        def gather(g, c):
            index = ghost_list[pl.ds(pl.multiple_of(g * LANES, LANES), LANES)].reshape(1, LANES)
            low = jnp.broadcast_to(index & (LANES - 1), (8, LANES))
            high = jnp.broadcast_to(index >> 7, (8, LANES))
            found = zeros8
            for t in range(TILES):
                here = jnp.take_along_axis(
                    own[8 * t : 8 * t + 8, :], low, axis=1, mode="promise_in_bounds"
                )
                found = jnp.where(high == t, here, found)
            ghost_out[step, g] = found
            return c

        lax.fori_loop(0, GHOST_TILES, gather, 0)
        for j in range(6):

            @pl.when(slots[j][3])
            def _():
                ghost_copy(step, j).start()

        coords = [dense(k) for k in range(3)]
        centred = [coords[0], coords[1], coords[2] + ((gz.astype(f32) + 0.5) * side - 0.5)]
        powers = monomials(centred)
        for m, triple in enumerate(TRIPLES):
            for k in range(3):
                term = dense_strength[k]
                if powers[triple] is not None:
                    term = term * powers[triple]
                folded = functools.reduce(lambda a, b: a + b, [term[8 * i : 8 * i + 8] for i in range(TILES // 8)])
                partial[8 * (4 * m + k) : 8 * (4 * m + k) + 8, :] = folded
            if step == 0:
                partial[8 * (4 * m + 3) : 8 * (4 * m + 3) + 8, :] = zeros8
        summed = None
        for i in range(8):
            rows = partial[pl.ds(i, 4 * COUNT, stride=8), :]
            summed = rows if summed is None else summed + rows
        summed = jnp.concatenate([summed, jnp.zeros((MESSAGE - 4 * COUNT, LANES), f32)], axis=0)
        ones = jnp.ones((8, 3 * LANES), bf16)
        parts = jnp.concatenate([p.astype(bf16) for p in split3(summed)], axis=1)
        part = lax.dot_general(ones, parts, (((1,), (1,)), ((), ())), preferred_element_type=f32)[0:1]
        message[step, 0] = part

        def send_column(d, c):
            column_copy(step, d).start()
            return c

        lax.fori_loop(1, deep, send_column, 0)

        def own_quad(q, c):
            tiles = []
            for u in range(4):
                t = 4 * q + u
                raw = own[pl.ds(pl.multiple_of(8 * t, 8), 8), :]
                tiles.append(raw)
                rows = jnp.concatenate(target_rows(raw), axis=0).astype(bf16)
                for quarter in range(4):
                    target_feat[4 * t + quarter, 32 * quarter : 32 * quarter + 32, :] = rows
                if step == 0:
                    source_str[t] = strength_rows(raw)
            source_quad(q, tiles)
            return c

        lax.fori_loop(0, TILES // 4, own_quad, 0)

        if step == 0:
            separation = (
                away_x.astype(f32),
                away_y.astype(f32),
                jnp.full((4, plane), (gz.astype(f32) + 0.5) * side - 0.5, f32),
            )
            for q, value in enumerate(derivatives(separation).values()):
                far_weights[4 * q : 4 * q + 4, :] = value

        all_column(step).wait_recv()
        total = message[step, 0]
        for d in range(1, deep):
            total = total + column_in[step, d - 1]
        message[step, 1] = total
        plane_in[step, rank] = total

        def send_plane(d, c):
            plane_copy(step, d).start()
            return c

        lax.fori_loop(1, plane, send_plane, 0)

        for j in range(6):

            @pl.when(slots[j][2])
            def _():
                ghost_copy(step, j).wait_recv()

            axis, offset = slots[j][0], slots[j][1]
            moved = jnp.where(sub == axis, offset, 0.0)

            def ghost_quad(q, c):
                tiles = []
                for u in range(4):
                    raw = ghost_in[step, j, 4 * q + u]
                    tiles.append(raw + moved)
                    if step == 0:
                        source_str[TILES + j * GHOST_TILES + 4 * q + u] = strength_rows(raw)
                source_quad(TILES // 4 + j * (GHOST_TILES // 4) + q, tiles)
                return c

            lax.fori_loop(0, GHOST_TILES // 4, ghost_quad, 0)

        def near(b, c):
            values = []
            for u in range(UNROLL):
                p = b * UNROLL + u
                t, s = targets[p], sources[p]
                gap = jnp.dot(source_feat[s >> 2], target_feat[4 * t + (s & 3)], preferred_element_type=f32)
                values.append(halves(lax.rsqrt(jnp.maximum(gap, core_sq))))
            for u in range(UNROLL):
                p = b * UNROLL + u
                pushed = source_str[sources[p]]
                pushed = jnp.concatenate([pushed, pushed], axis=1)
                both = jnp.concatenate(values[u], axis=0)
                contrib[pl.ds(pl.multiple_of(16 * p, 16), 16), :] = jnp.dot(
                    pushed, both, preferred_element_type=f32
                )
            return c

        lax.fori_loop(0, NPAIR // UNROLL, near, 0)
        velocity = []
        for k in range(3):
            rows = contrib[pl.ds(3 + k, NPAIR, stride=16), :] + contrib[pl.ds(11 + k, NPAIR, stride=16), :]
            both = jnp.concatenate(halves(rows), axis=0)
            velocity.append(jnp.dot(chosen, both, preferred_element_type=f32))

        all_plane(step).wait_recv()
        for s in range(plane):
            gathered[s : s + 1, :] = plane_in[step, s]
        turned[...] = jnp.transpose(gathered[...])
        expansion = {}
        for m, inner in enumerate(TRIPLES):
            factor = (-1.0) ** sum(inner) / factorial(inner)
            source = jnp.where(is_far, turned[4 * m : 4 * m + 4, :] * factor, 0.0)
            for outer in TRIPLES:
                if sum(outer) + sum(inner) <= ORDER:
                    q = PLACE[tuple(a + b for a, b in zip(outer, inner))]
                    term = far_weights[4 * q : 4 * q + 4, :] * source
                    expansion[outer] = term if outer not in expansion else expansion[outer] + term
        for n, outer in enumerate(TRIPLES):
            value = jnp.sum(expansion[outer], axis=1, keepdims=True) * (1.0 / factorial(outer))
            local[4 * n : 4 * n + 4, :] = jnp.broadcast_to(value, (4, LANES))
        powers = monomials(coords)
        for n, outer in enumerate(TRIPLES):
            for k in range(3):
                term = jnp.broadcast_to(local[4 * n + k : 4 * n + k + 1, :], (TILES, LANES))
                if powers[outer] is not None:
                    term = term * powers[outer]
                velocity[k] = velocity[k] + term

        if step == 0:
            centre = (gx.astype(f32) + 0.5, gy.astype(f32) + 0.5, (gz.astype(f32) + 0.5) * side)
            block_out[...] = jnp.zeros_like(block_out)
            for k in range(3):
                moved = coords[k] + time_step * velocity[k]
                own[pl.ds(k, TILES, stride=8), :] = moved
                place(0, k, moved + centre[k])
            send_blocks(0)

    for k in range(3):
        place(1, k, velocity[k])
    send_blocks(1)
    all_blocks(0).wait_recv()
    all_blocks(1).wait_recv()
    for s in range(plane):
        start = block_in[8 * s : 8 * s + 8, :]
        speed = block_in[8 * (plane + s) : 8 * (plane + s) + 8, :]
        ended = start + time_step * speed
        for r in range(CAP):
            out_pos[CAP * s + r] = ended[3 * r : 3 * r + 3]
            out_vel[CAP * s + r] = speed[3 * r : 3 * r + 3]

    for step in range(2):
        for j in range(6):

            @pl.when(slots[j][3])
            def _():
                ghost_copy(step, j).wait_send()

        all_column(step).wait_send()
        all_plane(step).wait_send()
        all_blocks(step).wait_send()


def per_device(offsets, strength, ghost_list, pair_targets, pair_sources, owners):
    sizes = tuple(lax.axis_size(axis) for axis in ("gx", "gy", "gz"))
    wide, tall, deep = sizes
    plane = wide * tall
    vmem = pl.BlockSpec(memory_space=pltpu.VMEM)
    smem = pl.BlockSpec(memory_space=pltpu.SMEM)
    shape = jax.ShapeDtypeStruct((plane * CAP, 3, LANES), f32)
    dma = pltpu.SemaphoreType.DMA
    return pl.pallas_call(
        functools.partial(kernel, sizes),
        out_shape=(shape, shape),
        in_specs=[vmem, vmem, vmem, smem, vmem, smem, vmem],
        out_specs=(vmem, vmem),
        scratch_shapes=[
            pltpu.VMEM((8 * TILES, LANES), f32),
            pltpu.VMEM((2, GHOST_TILES, 8, LANES), f32),
            pltpu.VMEM((2, 6, GHOST_TILES, 8, LANES), f32),
            pltpu.VMEM((4 * TILES, LANES, LANES), bf16),
            pltpu.VMEM((SOURCES // 4, LANES, LANES), bf16),
            pltpu.VMEM((SOURCES, 16, LANES), bf16),
            pltpu.VMEM((NPAIR * 16, LANES), f32),
            pltpu.VMEM((4 * COUNT * 8, LANES), f32),
            pltpu.VMEM((2, 2, 1, MESSAGE), f32),
            pltpu.VMEM((2, deep - 1, 1, MESSAGE), f32),
            pltpu.VMEM((2, plane, 1, MESSAGE), f32),
            pltpu.VMEM((plane, MESSAGE), f32),
            pltpu.VMEM((MESSAGE, plane), f32),
            pltpu.VMEM((4 * COUNT, LANES), f32),
            pltpu.VMEM((4 * COUNT, plane), f32),
            pltpu.VMEM((2 * plane * 8, LANES), f32),
            pltpu.VMEM((2 * plane * 8, LANES), f32),
            dma((2, 6)),
            dma((2, 6)),
            dma((2,)),
            dma((2,)),
            dma((2,)),
            dma((2,)),
            dma((2,)),
            dma((2,)),
        ],
        compiler_params=pltpu.CompilerParams(
            collective_id=0, has_side_effects=True, vmem_limit_bytes=40 << 20
        ),
        name="dislocation_steps",
    )(offsets, strength, ghost_list, pair_targets, pair_targets, pair_sources, owners)


def solution(mesh):
    return jax.shard_map(
        per_device,
        mesh=mesh,
        in_specs=(
            P(None, ("gx", "gy", "gz")),
            P(None, ("gx", "gy", "gz")),
            P(("gx", "gy", "gz")),
            P(("gx", "gy", "gz")),
            P(("gx", "gy", "gz")),
            P(("gx", "gy", "gz"), None),
        ),
        out_specs=(P(("gx", "gy", "gz"), None, None), P(("gx", "gy", "gz"), None, None)),
        check_vma=False,
    )
```

```python
import functools
import math

import jax
import jax.numpy as jnp
import numpy as np
from jax import lax
from jax.experimental import pallas as pl
from jax.experimental.pallas import tpu as pltpu
from jax.sharding import PartitionSpec as P

SEG = 4096
ORDER = 5
GHOST = 1536
NPAIR = 128
CAP = 2
LANES = 128
TILES = SEG // LANES
GHOST_TILES = GHOST // LANES
SOURCES = TILES + 6 * GHOST_TILES
UNROLL = 32

core_sq = 0.0025
time_step = 0.1
bf16 = jnp.bfloat16
f32 = jnp.float32
MESH = pl.DeviceIdType.MESH

TRIPLES = [
    (i, j, d - i - j)
    for d in range(ORDER + 1)
    for i in range(d, -1, -1)
    for j in range(d - i, -1, -1)
]
PLACE = {triple: at for at, triple in enumerate(TRIPLES)}
COUNT = len(TRIPLES)
MESSAGE = 256


def factorial(triple):
    return float(math.prod(math.factorial(e) for e in triple))


def lowered(triple, axis, by=1):
    out = list(triple)
    out[axis] -= by
    return tuple(out)


def monomials(coords):
    made = {}
    for triple in TRIPLES:
        if sum(triple) == 0:
            made[triple] = None
        else:
            axis = next(a for a in range(3) if triple[a])
            below = made[lowered(triple, axis)]
            made[triple] = coords[axis] if below is None else below * coords[axis]
    return made


def derivatives(separation):
    rx, ry, rz = separation
    inverse = 1.0 / (rx * rx + ry * ry + rz * rz + core_sq)
    taylor = {(0, 0, 0): lax.sqrt(inverse)}
    for triple in TRIPLES[1:]:
        n = sum(triple)
        first, second = None, None
        for axis in range(3):
            if triple[axis] >= 1:
                term = separation[axis] * taylor[lowered(triple, axis)]
                first = term if first is None else first + term
            if triple[axis] >= 2:
                term = taylor[lowered(triple, axis, 2)]
                second = term if second is None else second + term
        total = first * (-(2.0 * n - 1.0) / n)
        if second is not None:
            total = total - second * ((n - 1.0) / n)
        taylor[triple] = total * inverse
    return {t: v if factorial(t) == 1.0 else v * factorial(t) for t, v in taylor.items()}


def split3(value):
    high = value.astype(bf16).astype(f32)
    rest = value - high
    middle = rest.astype(bf16).astype(f32)
    return high, middle, rest - middle


def halves(value):
    high = value.astype(bf16)
    return high, (value - high.astype(f32)).astype(bf16)


def kernel(
    sizes,
    offsets_in, strength_in, ghost_list, targets, target_row, sources, owners,
    out_start, out_speed,
    offsets, strength, input_done,
    own, paired, ghost_out, ghost_in, ghost_out_late, ghost_in_late, target_feat, source_feat, source_str, contrib, partial,
    message, column_in, plane_in, gathered, turned, local, far_weights, block_out, block_in,
    ghost_send, ghost_recv, column_send, column_recv, plane_send, plane_recv, block_send, block_recv,
):
    wide, tall, deep = sizes
    plane = wide * tall
    gx, gy, gz = lax.axis_index("gx"), lax.axis_index("gy"), lax.axis_index("gz")
    rank = gx * tall + gy
    shift = tall.bit_length() - 1
    side = 1.0 / deep
    sub = lax.broadcasted_iota(jnp.int32, (8, LANES), 0)

    def along(d):
        return (gx, gy, (gz + d) & (deep - 1))

    def across(d):
        other = (rank + d) & (plane - 1)
        return (other >> shift, other & (tall - 1), gz)

    load_offsets = pltpu.make_async_copy(offsets_in, offsets, input_done.at[0])
    load_strength = pltpu.make_async_copy(strength_in, strength, input_done.at[1])
    load_offsets.start()
    load_strength.start()

    barrier = pltpu.get_barrier_semaphore()

    def greet_column(d, c):
        pl.semaphore_signal(barrier, inc=1, device_id=along(d), device_id_type=MESH)
        return c

    def greet_plane(d, c):
        pl.semaphore_signal(barrier, inc=1, device_id=across(d), device_id_type=MESH)
        return c

    lax.fori_loop(1, deep, greet_column, 0)
    lax.fori_loop(1, plane, greet_plane, 0)

    position = (gx, gy, gz)
    slots = []
    for axis, count in enumerate((wide, tall, deep)):
        at = position[axis]
        up = tuple(p + 1 if i == axis else p for i, p in enumerate(position))
        down = tuple(p - 1 if i == axis else p for i, p in enumerate(position))
        step = side if axis == 2 else 1.0
        slots.append((axis, -step, at > 0, at < count - 1, up))
        slots.append((axis, step, at < count - 1, at > 0, down))

    scale = jnp.where(lax.broadcasted_iota(jnp.int32, (3, LANES), 0) == 2, side, 1.0)
    own[...] = jnp.zeros_like(own)
    target_feat[...] = jnp.zeros_like(target_feat)
    block_out[...] = jnp.zeros_like(block_out)
    load_offsets.wait()
    load_strength.wait()
    for t in range(TILES):
        lanes = slice(t * LANES, (t + 1) * LANES)
        own[8 * t : 8 * t + 3, :] = (offsets[:, lanes] - 0.5) * scale
        own[8 * t + 3 : 8 * t + 6, :] = strength[:, lanes]

    def dense(row):
        return own[pl.ds(row, TILES, stride=8), :]

    dense_strength = [dense(3 + k) for k in range(3)]

    lane = lax.broadcasted_iota(jnp.int32, (4, plane), 1)
    source_x, source_y = lane >> shift, lane & (tall - 1)
    away_x, away_y = gx - source_x, gy - source_y
    is_far = jnp.maximum(jnp.abs(away_x), jnp.abs(away_y)) >= 3

    rows_i = lax.broadcasted_iota(jnp.int32, (TILES, TILES), 0)
    cols_i = lax.broadcasted_iota(jnp.int32, (TILES, TILES), 1)
    row_f = owners[...].astype(f32)
    column_f = jnp.sum(jnp.where(rows_i == cols_i, row_f, 0.0), axis=1, keepdims=True)
    earlier = jnp.where((column_f == row_f) & (rows_i < cols_i), 1.0, 0.0)
    slot_f = jnp.sum(earlier, axis=0, keepdims=True) * plane + row_f
    slot_rows = lax.broadcasted_iota(jnp.int32, (CAP * plane, TILES), 0).astype(f32)
    placer = jnp.where(slot_rows == slot_f, 1.0, 0.0).astype(bf16)
    placer = jnp.concatenate([placer, placer, placer], axis=1)

    def place(which, k, field):
        parts = jnp.concatenate([p.astype(bf16) for p in split3(field)], axis=0)
        placed = jnp.dot(placer, parts, preferred_element_type=f32)
        for r in range(CAP):
            rows = pl.ds(which * plane * 8 + 3 * r + k, plane, stride=8)
            block_out[rows, :] = placed[r * plane : (r + 1) * plane]

    def block_rows(which, o):
        return pl.ds(pl.multiple_of(which * plane * 8 + 8 * o, 8), 8)

    def block_copy(which, d):
        target = across(d)
        other = target[0] * tall + target[1]
        return pltpu.make_async_remote_copy(
            src_ref=block_out.at[block_rows(which, other)],
            dst_ref=block_in.at[block_rows(which, rank)],
            send_sem=block_send.at[which],
            recv_sem=block_recv.at[which],
            device_id=target,
            device_id_type=MESH,
        )

    def send_blocks(which):
        def send(d, c):
            block_copy(which, d).start()
            return c

        lax.fori_loop(1, plane, send, 0)
        block_in[block_rows(which, rank), :] = block_out[block_rows(which, rank), :]

    def all_blocks(which):
        rows = pl.ds(which * plane * 8, (plane - 1) * 8)
        return pltpu.make_async_remote_copy(
            src_ref=block_out.at[rows],
            dst_ref=block_in.at[rows],
            send_sem=block_send.at[which],
            recv_sem=block_recv.at[which],
            device_id=across(1),
            device_id_type=MESH,
        )

    def ghost_copy(step, j):
        return pltpu.make_async_remote_copy(
            src_ref=ghost_out if step == 0 else ghost_out_late,
            dst_ref=ghost_in.at[j] if step == 0 else ghost_in_late.at[j],
            send_sem=ghost_send.at[step, j],
            recv_sem=ghost_recv.at[step, j],
            device_id=slots[j][4],
            device_id_type=MESH,
        )

    def column_copy(step, d):
        return pltpu.make_async_remote_copy(
            src_ref=message.at[step, 0],
            dst_ref=column_in.at[step, d - 1],
            send_sem=column_send.at[step],
            recv_sem=column_recv.at[step],
            device_id=along(d),
            device_id_type=MESH,
        )

    def all_column(step):
        return pltpu.make_async_remote_copy(
            src_ref=column_in.at[step],
            dst_ref=column_in.at[step],
            send_sem=column_send.at[step],
            recv_sem=column_recv.at[step],
            device_id=along(1),
            device_id_type=MESH,
        )

    def plane_copy(step, d):
        return pltpu.make_async_remote_copy(
            src_ref=message.at[step, 1],
            dst_ref=plane_in.at[step, rank],
            send_sem=plane_send.at[step],
            recv_sem=plane_recv.at[step],
            device_id=across(d),
            device_id_type=MESH,
        )

    def all_plane(step):
        rows = plane_in.at[step, pl.ds(0, plane - 1)]
        return pltpu.make_async_remote_copy(
            src_ref=rows,
            dst_ref=rows,
            send_sem=plane_send.at[step],
            recv_sem=plane_recv.at[step],
            device_id=across(1),
            device_id_type=MESH,
        )

    for j in range(6):

        @pl.when(jnp.logical_not(slots[j][2]))
        def _():
            ghost_in[j] = jnp.zeros((GHOST_TILES, 8, LANES), f32)
            ghost_in_late[j] = jnp.zeros((GHOST_TILES // 2, 8, LANES), f32)

    centre = (gx.astype(f32) + 0.5, gy.astype(f32) + 0.5, (gz.astype(f32) + 0.5) * side)
    zeros8 = jnp.zeros((8, LANES), f32)

    def squares(raw):
        return jnp.sum(jnp.where(sub < 3, raw * raw, 0.0), axis=0, keepdims=True)

    def source_rows(raw):
        mixed = jnp.where(sub < 3, raw, jnp.where(sub < 6, pltpu.roll(raw, 3, 0), 1.0))
        value = jnp.where(sub == 6, squares(raw), mixed)
        high, middle, low = split3(value)
        return [
            high,
            jnp.where(sub == 7, high, middle),
            jnp.where((sub < 3) | (sub == 6), low, high),
            zeros8,
        ]

    def target_rows(raw):
        mixed = jnp.where(sub < 3, -2.0 * raw, jnp.where(sub < 6, -2.0 * pltpu.roll(raw, 3, 0), 1.0))
        value = jnp.where(sub == 7, squares(raw) + core_sq, mixed)
        high, middle, low = split3(value)
        second = (sub >= 3) & (sub < 6)
        last = second | (sub == 7)
        return [
            jnp.where(second, middle, high),
            jnp.where(last, middle, high),
            jnp.where(last, low, high),
            zeros8,
        ]

    def strength_rows(raw):
        high = raw.astype(bf16).astype(f32)
        return jnp.concatenate([high, raw - high], axis=0).astype(bf16)

    def source_quad(quad, tiles):
        rows = [row for raw in tiles for row in source_rows(raw)]
        source_feat[quad] = jnp.transpose(jnp.concatenate(rows, axis=0)).astype(bf16)

    chosen = (lax.broadcasted_iota(jnp.int32, (TILES, NPAIR), 0) == target_row[...].reshape(1, NPAIR))
    chosen = jnp.where(chosen, 1.0, 0.0).astype(bf16)
    chosen = jnp.concatenate([chosen, chosen], axis=1)

    def ghost_index(g):
        index = ghost_list[pl.ds(pl.multiple_of(g * LANES, LANES), LANES)].reshape(1, LANES)
        return jnp.broadcast_to(index & (LANES - 1), (8, LANES)), jnp.broadcast_to(index >> 7, (8, LANES))

    def take(tile, low):
        return jnp.take_along_axis(tile, low, axis=1, mode="promise_in_bounds")

    def gather_all(step):
        def whole(g, c):
            low, high = ghost_index(g)
            found = zeros8
            for t in range(TILES):
                found = jnp.where(high == t, take(own[8 * t : 8 * t + 8, :], low), found)
            ghost_out[g] = found
            return c

        def pair(g, c):
            both = []
            for u in range(2):
                low, high = ghost_index(2 * g + u)
                high = high - (sub >> 2)
                found = zeros8
                for t in range(TILES // 2):
                    found = jnp.where(high == 2 * t, take(paired[t], low), found)
                both.append(found + pltpu.roll(found, 4, 0))
            ghost_out_late[g] = jnp.where(sub < 4, both[0], both[1])
            return c

        if step == 0:
            lax.fori_loop(0, GHOST_TILES, whole, 0)
        else:
            for t in range(TILES // 2):
                first, second = own[16 * t : 16 * t + 8, :], own[16 * t + 8 : 16 * t + 16, :]
                paired[t] = jnp.where(sub < 4, first, pltpu.roll(second, 4, 0))
            lax.fori_loop(0, GHOST_TILES // 2, pair, 0)

    def send_ghosts(step):
        for j in range(6):

            @pl.when(slots[j][3])
            def _():
                ghost_copy(step, j).start()

    velocity = None
    for step in range(2):

        gather_all(step)
        if step == 1:
            send_ghosts(step)

        coords = [dense(k) for k in range(3)]
        centred = [coords[0], coords[1], coords[2] + ((gz.astype(f32) + 0.5) * side - 0.5)]
        powers = monomials(centred)
        for m, triple in enumerate(TRIPLES):
            for k in range(3):
                term = dense_strength[k]
                if powers[triple] is not None:
                    term = term * powers[triple]
                folded = functools.reduce(lambda a, b: a + b, [term[8 * i : 8 * i + 8] for i in range(TILES // 8)])
                partial[8 * (4 * m + k) : 8 * (4 * m + k) + 8, :] = folded
            if step == 0:
                partial[8 * (4 * m + 3) : 8 * (4 * m + 3) + 8, :] = zeros8
        summed = None
        for i in range(8):
            rows = partial[pl.ds(i, 4 * COUNT, stride=8), :]
            summed = rows if summed is None else summed + rows
        summed = jnp.concatenate([summed, jnp.zeros((MESSAGE - 4 * COUNT, LANES), f32)], axis=0)
        ones = jnp.ones((8, 3 * LANES), bf16)
        parts = jnp.concatenate([p.astype(bf16) for p in split3(summed)], axis=1)
        part = lax.dot_general(ones, parts, (((1,), (1,)), ((), ())), preferred_element_type=f32)[0:1]
        message[step, 0] = part

        def send_column(d, c):
            column_copy(step, d).start()
            return c

        if step == 1:
            lax.fori_loop(1, deep, send_column, 0)

        def own_quads(i, c):
            for v in range(4):
                own_quad(4 * i + v)
            return c

        def own_quad(q):
            tiles = []
            for u in range(4):
                t = 4 * q + u
                raw = own[pl.ds(pl.multiple_of(8 * t, 8), 8), :]
                tiles.append(raw)
                rows = jnp.concatenate(target_rows(raw), axis=0).astype(bf16)
                for quarter in range(4):
                    target_feat[4 * t + quarter, 32 * quarter : 32 * quarter + 32, :] = rows
                if step == 0:
                    source_str[t] = strength_rows(raw)
            source_quad(q, tiles)

        lax.fori_loop(0, TILES // 16, own_quads, 0)

        if step == 0:
            separation = (
                away_x.astype(f32),
                away_y.astype(f32),
                jnp.full((4, plane), (gz.astype(f32) + 0.5) * side - 0.5, f32),
            )
            for q, value in enumerate(derivatives(separation).values()):
                far_weights[4 * q : 4 * q + 4, :] = value

            pl.semaphore_wait(barrier, deep - 1 + plane - 1)
            send_ghosts(step)
            lax.fori_loop(1, deep, send_column, 0)
        else:
            for k in range(3):
                place(0, k, coords[k] + centre[k])
            send_blocks(0)

        all_column(step).wait_recv()
        total = message[step, 0]
        for d in range(1, deep):
            total = total + column_in[step, d - 1]
        message[step, 1] = total
        plane_in[step, rank] = total

        def send_plane(d, c):
            plane_copy(step, d).start()
            return c

        lax.fori_loop(1, plane, send_plane, 0)

        for j in range(6):

            @pl.when(slots[j][2])
            def _():
                ghost_copy(step, j).wait_recv()

            axis, offset = slots[j][0], slots[j][1]
            moved = jnp.where(sub == axis, offset, 0.0)

            for q in range(GHOST_TILES // 4):
                tiles = []
                for u in range(4):
                    g = 4 * q + u
                    if step == 0:
                        raw = ghost_in[j, g]
                        source_str[TILES + j * GHOST_TILES + g] = strength_rows(raw)
                    elif u % 2 == 0:
                        raw = ghost_in_late[j, g // 2]
                    else:
                        raw = pltpu.roll(ghost_in_late[j, g // 2], 4, 0)
                    tiles.append(raw + moved)
                source_quad(TILES // 4 + j * (GHOST_TILES // 4) + q, tiles)

        def near(b, c):
            values = []
            for u in range(UNROLL):
                p = b * UNROLL + u
                t, s = targets[p], sources[p]
                gap = jnp.dot(source_feat[s >> 2], target_feat[4 * t + (s & 3)], preferred_element_type=f32)
                values.append(halves(lax.rsqrt(jnp.maximum(gap, core_sq))))
            for u in range(UNROLL):
                p = b * UNROLL + u
                pushed = source_str[sources[p]]
                pushed = jnp.concatenate([pushed, pushed], axis=1)
                both = jnp.concatenate(values[u], axis=0)
                contrib[pl.ds(pl.multiple_of(16 * p, 16), 16), :] = jnp.dot(
                    pushed, both, preferred_element_type=f32
                )
            return c

        lax.fori_loop(0, NPAIR // UNROLL, near, 0)
        velocity = []
        for k in range(3):
            rows = contrib[pl.ds(3 + k, NPAIR, stride=16), :] + contrib[pl.ds(11 + k, NPAIR, stride=16), :]
            both = jnp.concatenate(halves(rows), axis=0)
            velocity.append(jnp.dot(chosen, both, preferred_element_type=f32))

        all_plane(step).wait_recv()
        for s in range(plane):
            gathered[s : s + 1, :] = plane_in[step, s]
        turned[...] = jnp.transpose(gathered[...])
        expansion = {}
        for m, inner in enumerate(TRIPLES):
            factor = (-1.0) ** sum(inner) / factorial(inner)
            source = jnp.where(is_far, turned[4 * m : 4 * m + 4, :] * factor, 0.0)
            for outer in TRIPLES:
                if sum(outer) + sum(inner) <= ORDER:
                    q = PLACE[tuple(a + b for a, b in zip(outer, inner))]
                    term = far_weights[4 * q : 4 * q + 4, :] * source
                    expansion[outer] = term if outer not in expansion else expansion[outer] + term
        for n, outer in enumerate(TRIPLES):
            value = jnp.sum(expansion[outer], axis=1, keepdims=True) * (1.0 / factorial(outer))
            local[4 * n : 4 * n + 4, :] = jnp.broadcast_to(value, (4, LANES))
        powers = monomials(coords)
        for n, outer in enumerate(TRIPLES):
            for k in range(3):
                term = jnp.broadcast_to(local[4 * n + k : 4 * n + k + 1, :], (TILES, LANES))
                if powers[outer] is not None:
                    term = term * powers[outer]
                velocity[k] = velocity[k] + term

        if step == 0:
            for k in range(3):
                own[pl.ds(k, TILES, stride=8), :] = coords[k] + time_step * velocity[k]

    for k in range(3):
        place(1, k, velocity[k])
    send_blocks(1)
    all_blocks(0).wait_recv()
    all_blocks(1).wait_recv()
    for which, out in ((0, out_start), (1, out_speed)):
        for k in range(3):
            for r in range(CAP):
                rows = pl.ds(which * plane * 8 + 3 * r + k, plane, stride=8)
                out[k, pl.ds(r, plane, stride=CAP), :] = block_in[rows, :]

    for step in range(2):
        for j in range(6):

            @pl.when(slots[j][3])
            def _():
                ghost_copy(step, j).wait_send()

        all_column(step).wait_send()
        all_plane(step).wait_send()
        all_blocks(step).wait_send()


def finish(start, speed):
    moved = start + time_step * speed
    return moved.transpose(1, 0, 2), speed.transpose(1, 0, 2)


def per_device(offsets, strength, ghost_list, pair_targets, pair_sources, owners):
    sizes = tuple(lax.axis_size(axis) for axis in ("gx", "gy", "gz"))
    wide, tall, deep = sizes
    plane = wide * tall
    vmem = pl.BlockSpec(memory_space=pltpu.VMEM)
    smem = pl.BlockSpec(memory_space=pltpu.SMEM)
    hbm = pl.BlockSpec(memory_space=pltpu.HBM)
    shape = jax.ShapeDtypeStruct((3, plane * CAP, LANES), f32)
    dma = pltpu.SemaphoreType.DMA
    start, speed = pl.pallas_call(
        functools.partial(kernel, sizes),
        out_shape=(shape, shape),
        in_specs=[hbm, hbm, vmem, smem, vmem, smem, vmem],
        out_specs=(vmem, vmem),
        scratch_shapes=[
            pltpu.VMEM((3, SEG), f32),
            pltpu.VMEM((3, SEG), f32),
            pltpu.SemaphoreType.DMA((2,)),
            pltpu.VMEM((8 * TILES, LANES), f32),
            pltpu.VMEM((TILES // 2, 8, LANES), f32),
            pltpu.VMEM((GHOST_TILES, 8, LANES), f32),
            pltpu.VMEM((6, GHOST_TILES, 8, LANES), f32),
            pltpu.VMEM((GHOST_TILES // 2, 8, LANES), f32),
            pltpu.VMEM((6, GHOST_TILES // 2, 8, LANES), f32),
            pltpu.VMEM((4 * TILES, LANES, LANES), bf16),
            pltpu.VMEM((SOURCES // 4, LANES, LANES), bf16),
            pltpu.VMEM((SOURCES, 16, LANES), bf16),
            pltpu.VMEM((NPAIR * 16, LANES), f32),
            pltpu.VMEM((4 * COUNT * 8, LANES), f32),
            pltpu.VMEM((2, 2, 1, MESSAGE), f32),
            pltpu.VMEM((2, deep - 1, 1, MESSAGE), f32),
            pltpu.VMEM((2, plane, 1, MESSAGE), f32),
            pltpu.VMEM((plane, MESSAGE), f32),
            pltpu.VMEM((MESSAGE, plane), f32),
            pltpu.VMEM((4 * COUNT, LANES), f32),
            pltpu.VMEM((4 * COUNT, plane), f32),
            pltpu.VMEM((2 * plane * 8, LANES), f32),
            pltpu.VMEM((2 * plane * 8, LANES), f32),
            dma((2, 6)),
            dma((2, 6)),
            dma((2,)),
            dma((2,)),
            dma((2,)),
            dma((2,)),
            dma((2,)),
            dma((2,)),
        ],
        compiler_params=pltpu.CompilerParams(
            collective_id=0, has_side_effects=True, vmem_limit_bytes=62 << 20
        ),
        name="dislocation_steps",
    )(offsets, strength, ghost_list, pair_targets, pair_targets, pair_sources, owners.reshape(1, TILES))
    return finish(start, speed)


def solution(mesh):
    return jax.shard_map(
        per_device,
        mesh=mesh,
        in_specs=(
            P(None, ("gx", "gy", "gz")),
            P(None, ("gx", "gy", "gz")),
            P(("gx", "gy", "gz")),
            P(("gx", "gy", "gz")),
            P(("gx", "gy", "gz")),
            P(("gx", "gy", "gz"), None),
        ),
        out_specs=(P(("gx", "gy", "gz"), None, None), P(("gx", "gy", "gz"), None, None)),
        check_vma=False,
    )
```

```python
import functools
import math

import jax
import jax.numpy as jnp
import numpy as np
from jax import lax
from jax.experimental import pallas as pl
from jax.experimental.pallas import tpu as pltpu
from jax.sharding import PartitionSpec as P

SEG = 4096
ORDER = 5
GHOST = 1536
NPAIR = 128
CAP = 2
LANES = 128
TILES = SEG // LANES
GHOST_TILES = GHOST // LANES
SOURCES = TILES + 6 * GHOST_TILES
UNROLL = 32

core_sq = 0.0025
time_step = 0.1
bf16 = jnp.bfloat16
f32 = jnp.float32
MESH = pl.DeviceIdType.MESH

TRIPLES = [
    (i, j, d - i - j)
    for d in range(ORDER + 1)
    for i in range(d, -1, -1)
    for j in range(d - i, -1, -1)
]
PLACE = {triple: at for at, triple in enumerate(TRIPLES)}
COUNT = len(TRIPLES)
MESSAGE = 256


def factorial(triple):
    return float(math.prod(math.factorial(e) for e in triple))


def lowered(triple, axis, by=1):
    out = list(triple)
    out[axis] -= by
    return tuple(out)


def monomials(coords):
    made = {}
    for triple in TRIPLES:
        if sum(triple) == 0:
            made[triple] = None
        else:
            axis = next(a for a in range(3) if triple[a])
            below = made[lowered(triple, axis)]
            made[triple] = coords[axis] if below is None else below * coords[axis]
    return made


def derivatives(separation):
    rx, ry, rz = separation
    inverse = 1.0 / (rx * rx + ry * ry + rz * rz + core_sq)
    taylor = {(0, 0, 0): lax.sqrt(inverse)}
    for triple in TRIPLES[1:]:
        n = sum(triple)
        first, second = None, None
        for axis in range(3):
            if triple[axis] >= 1:
                term = separation[axis] * taylor[lowered(triple, axis)]
                first = term if first is None else first + term
            if triple[axis] >= 2:
                term = taylor[lowered(triple, axis, 2)]
                second = term if second is None else second + term
        total = first * (-(2.0 * n - 1.0) / n)
        if second is not None:
            total = total - second * ((n - 1.0) / n)
        taylor[triple] = total * inverse
    return {t: v if factorial(t) == 1.0 else v * factorial(t) for t, v in taylor.items()}


def split3(value):
    high = value.astype(bf16).astype(f32)
    rest = value - high
    middle = rest.astype(bf16).astype(f32)
    return high, middle, rest - middle


def halves(value):
    high = value.astype(bf16)
    return high, (value - high.astype(f32)).astype(bf16)


def kernel(
    sizes,
    offsets_in, strength_in, ghost_list, targets, target_row, sources, owners,
    out_start, out_speed,
    offsets, strength, input_done,
    own, paired, ghost_out, ghost_in, ghost_out_late, ghost_in_late, target_feat, source_feat, source_str, contrib, partial,
    message, column_in, plane_in, gathered, turned, local, far_weights,
    start_flat, start_out, start_mid, start_in, speed_out, speed_in,
    ghost_send, ghost_recv, column_send, column_recv, plane_send, plane_recv, block_send, block_recv,
):
    wide, tall, deep = sizes
    plane = wide * tall
    gx, gy, gz = lax.axis_index("gx"), lax.axis_index("gy"), lax.axis_index("gz")
    rank = gx * tall + gy
    shift = tall.bit_length() - 1
    side = 1.0 / deep
    sub = lax.broadcasted_iota(jnp.int32, (8, LANES), 0)

    def along(d):
        return (gx, gy, (gz + d) & (deep - 1))

    def across(d):
        return ((gx + d[0]) & (wide - 1), (gy + d[1]) & (tall - 1), gz)

    def hops(d):
        return min(d[0], wide - d[0]) + min(d[1], tall - d[1])

    others = [(x, y) for x in range(wide) for y in range(tall) if x + y > 0]
    others.sort(key=hops, reverse=True)

    load_offsets = pltpu.make_async_copy(offsets_in, offsets, input_done.at[0])
    load_strength = pltpu.make_async_copy(strength_in, strength, input_done.at[1])
    load_offsets.start()
    load_strength.start()

    def along_y(d):
        return (gx, (gy + d) & (tall - 1), gz)

    def along_x(d):
        return ((gx + d) & (wide - 1), gy, gz)

    barrier = pltpu.get_barrier_semaphore()

    partners = [across(d) for d in others] + [along(d) for d in range(1, deep)]
    for partner in partners:
        pl.semaphore_signal(barrier, inc=1, device_id=partner, device_id_type=MESH)

    position = (gx, gy, gz)
    slots = []
    for axis, count in enumerate((wide, tall, deep)):
        at = position[axis]
        up = tuple(p + 1 if i == axis else p for i, p in enumerate(position))
        down = tuple(p - 1 if i == axis else p for i, p in enumerate(position))
        step = side if axis == 2 else 1.0
        slots.append((axis, -step, at > 0, at < count - 1, up))
        slots.append((axis, step, at < count - 1, at > 0, down))

    scale = jnp.where(lax.broadcasted_iota(jnp.int32, (3, LANES), 0) == 2, side, 1.0)
    own[...] = jnp.zeros_like(own)
    target_feat[...] = jnp.zeros_like(target_feat)
    start_flat[...] = jnp.zeros_like(start_flat)
    speed_out[...] = jnp.zeros_like(speed_out)
    load_offsets.wait()
    load_strength.wait()
    for t in range(TILES):
        lanes = slice(t * LANES, (t + 1) * LANES)
        own[8 * t : 8 * t + 3, :] = (offsets[:, lanes] - 0.5) * scale
        own[8 * t + 3 : 8 * t + 6, :] = strength[:, lanes]

    def dense(row):
        return own[pl.ds(row, TILES, stride=8), :]

    dense_strength = [dense(3 + k) for k in range(3)]

    lane = lax.broadcasted_iota(jnp.int32, (4, plane), 1)
    source_x, source_y = lane >> shift, lane & (tall - 1)
    away_x, away_y = gx - source_x, gy - source_y
    is_far = jnp.maximum(jnp.abs(away_x), jnp.abs(away_y)) >= 3

    rows_i = lax.broadcasted_iota(jnp.int32, (TILES, TILES), 0)
    cols_i = lax.broadcasted_iota(jnp.int32, (TILES, TILES), 1)
    row_f = owners[...].astype(f32)
    column_f = jnp.sum(jnp.where(rows_i == cols_i, row_f, 0.0), axis=1, keepdims=True)
    earlier = jnp.where((column_f == row_f) & (rows_i < cols_i), 1.0, 0.0)
    nth_f = jnp.sum(earlier, axis=0, keepdims=True) * plane
    slot_rows = lax.broadcasted_iota(jnp.int32, (CAP * plane, TILES), 0).astype(f32)

    def placer_of(order_f):
        placer = jnp.where(slot_rows == nth_f + order_f, 1.0, 0.0).astype(bf16)
        return jnp.concatenate([placer, placer, placer], axis=1)

    row_i = owners[...]
    placer_start = placer_of(((row_i & (tall - 1)) * wide + (row_i >> shift)).astype(f32))
    placer_speed = placer_of(row_f)

    def place(placer, out, k, field):
        parts = jnp.concatenate([p.astype(bf16) for p in split3(field)], axis=0)
        placed = jnp.dot(placer, parts, preferred_element_type=f32)
        for r in range(CAP):
            out[pl.ds(3 * r + k, plane, stride=8), :] = placed[r * plane : (r + 1) * plane]

    def remote(src, dst, send_sem, recv_sem, device):
        return pltpu.make_async_remote_copy(
            src_ref=src,
            dst_ref=dst,
            send_sem=send_sem,
            recv_sem=recv_sem,
            device_id=device,
            device_id_type=MESH,
        )

    def speed_rows(o):
        return pl.ds(pl.multiple_of(8 * o, 8), 3 * CAP)

    def speed_copy(d):
        target = across(d)
        other = target[0] * tall + target[1]
        return remote(
            speed_out.at[speed_rows(other)], speed_in.at[speed_rows(rank)], block_send.at[0], block_recv.at[0], target
        )

    def all_speed():
        rows = pl.ds(0, (plane - 1) * 3 * CAP)
        return remote(speed_out.at[rows], speed_in.at[rows], block_send.at[0], block_recv.at[0], across(others[0]))

    def start_y_copy(d):
        target = along_y(d)
        return remote(
            start_out.at[target[1]], start_mid.at[:, gy], block_send.at[1], block_recv.at[1], target
        )

    def all_start_y():
        part = start_mid.at[:, pl.ds(0, tall - 1)]
        return remote(part, part, block_send.at[1], block_recv.at[1], along_y(1))

    def start_x_copy(d):
        target = along_x(d)
        return remote(
            start_mid.at[target[0]], start_in.at[gx], block_send.at[2], block_recv.at[2], target
        )

    def all_start_x():
        part = start_in.at[pl.ds(0, wide - 1)]
        return remote(part, part, block_send.at[2], block_recv.at[2], along_x(1))

    def ghost_copy(step, j):
        return pltpu.make_async_remote_copy(
            src_ref=ghost_out if step == 0 else ghost_out_late,
            dst_ref=ghost_in.at[j] if step == 0 else ghost_in_late.at[j],
            send_sem=ghost_send.at[step, j],
            recv_sem=ghost_recv.at[step, j],
            device_id=slots[j][4],
            device_id_type=MESH,
        )

    def column_copy(step, d):
        return pltpu.make_async_remote_copy(
            src_ref=message.at[step, 0],
            dst_ref=column_in.at[step, d - 1],
            send_sem=column_send.at[step],
            recv_sem=column_recv.at[step],
            device_id=along(d),
            device_id_type=MESH,
        )

    def all_column(step):
        return pltpu.make_async_remote_copy(
            src_ref=column_in.at[step],
            dst_ref=column_in.at[step],
            send_sem=column_send.at[step],
            recv_sem=column_recv.at[step],
            device_id=along(1),
            device_id_type=MESH,
        )

    def plane_copy(step, d):
        return remote(
            message.at[step, 1], plane_in.at[step, rank], plane_send.at[step], plane_recv.at[step], across(d)
        )

    def all_plane(step):
        rows = plane_in.at[step, pl.ds(0, plane - 1)]
        return remote(rows, rows, plane_send.at[step], plane_recv.at[step], across(others[0]))

    for j in range(6):

        @pl.when(jnp.logical_not(slots[j][2]))
        def _():
            ghost_in[j] = jnp.zeros((GHOST_TILES, 8, LANES), f32)
            ghost_in_late[j] = jnp.zeros((GHOST_TILES // 2, 8, LANES), f32)

    centre = (gx.astype(f32) + 0.5, gy.astype(f32) + 0.5, (gz.astype(f32) + 0.5) * side)
    zeros8 = jnp.zeros((8, LANES), f32)

    def squares(raw):
        return jnp.sum(jnp.where(sub < 3, raw * raw, 0.0), axis=0, keepdims=True)

    def source_rows(raw):
        mixed = jnp.where(sub < 3, raw, jnp.where(sub < 6, pltpu.roll(raw, 3, 0), 1.0))
        value = jnp.where(sub == 6, squares(raw), mixed)
        high, middle, low = split3(value)
        return [
            high,
            jnp.where(sub == 7, high, middle),
            jnp.where((sub < 3) | (sub == 6), low, high),
            zeros8,
        ]

    def target_rows(raw):
        mixed = jnp.where(sub < 3, -2.0 * raw, jnp.where(sub < 6, -2.0 * pltpu.roll(raw, 3, 0), 1.0))
        value = jnp.where(sub == 7, squares(raw) + core_sq, mixed)
        high, middle, low = split3(value)
        second = (sub >= 3) & (sub < 6)
        last = second | (sub == 7)
        return [
            jnp.where(second, middle, high),
            jnp.where(last, middle, high),
            jnp.where(last, low, high),
            zeros8,
        ]

    def strength_rows(raw):
        high = raw.astype(bf16).astype(f32)
        return jnp.concatenate([high, raw - high], axis=0).astype(bf16)

    def source_quad(quad, tiles):
        rows = [row for raw in tiles for row in source_rows(raw)]
        source_feat[quad] = jnp.transpose(jnp.concatenate(rows, axis=0)).astype(bf16)

    chosen = (lax.broadcasted_iota(jnp.int32, (TILES, NPAIR), 0) == target_row[...].reshape(1, NPAIR))
    chosen = jnp.where(chosen, 1.0, 0.0).astype(bf16)
    chosen = jnp.concatenate([chosen, chosen], axis=1)

    def ghost_index(g):
        index = ghost_list[pl.ds(pl.multiple_of(g * LANES, LANES), LANES)].reshape(1, LANES)
        return jnp.broadcast_to(index & (LANES - 1), (8, LANES)), jnp.broadcast_to(index >> 7, (8, LANES))

    def take(tile, low):
        return jnp.take_along_axis(tile, low, axis=1, mode="promise_in_bounds")

    def gather_all(step):
        def whole(g, c):
            low, high = ghost_index(g)
            found = zeros8
            for t in range(TILES):
                found = jnp.where(high == t, take(own[8 * t : 8 * t + 8, :], low), found)
            ghost_out[g] = found
            return c

        def pair(g, c):
            both = []
            for u in range(2):
                low, high = ghost_index(2 * g + u)
                high = high - (sub >> 2)
                found = zeros8
                for t in range(TILES // 2):
                    found = jnp.where(high == 2 * t, take(paired[t], low), found)
                both.append(found + pltpu.roll(found, 4, 0))
            ghost_out_late[g] = jnp.where(sub < 4, both[0], both[1])
            return c

        if step == 0:
            lax.fori_loop(0, GHOST_TILES, whole, 0)
        else:
            for t in range(TILES // 2):
                first, second = own[16 * t : 16 * t + 8, :], own[16 * t + 8 : 16 * t + 16, :]
                paired[t] = jnp.where(sub < 4, first, pltpu.roll(second, 4, 0))
            lax.fori_loop(0, GHOST_TILES // 2, pair, 0)

    def send_ghosts(step):
        for j in range(6):

            @pl.when(slots[j][3])
            def _():
                ghost_copy(step, j).start()

    velocity = None
    for step in range(2):

        coords = [dense(k) for k in range(3)]
        centred = [coords[0], coords[1], coords[2] + ((gz.astype(f32) + 0.5) * side - 0.5)]
        powers = monomials(centred)
        for m, triple in enumerate(TRIPLES):
            for k in range(3):
                term = dense_strength[k]
                if powers[triple] is not None:
                    term = term * powers[triple]
                folded = functools.reduce(lambda a, b: a + b, [term[8 * i : 8 * i + 8] for i in range(TILES // 8)])
                partial[8 * (4 * m + k) : 8 * (4 * m + k) + 8, :] = folded
            if step == 0:
                partial[8 * (4 * m + 3) : 8 * (4 * m + 3) + 8, :] = zeros8
        summed = None
        for i in range(8):
            rows = partial[pl.ds(i, 4 * COUNT, stride=8), :]
            summed = rows if summed is None else summed + rows
        summed = jnp.concatenate([summed, jnp.zeros((MESSAGE - 4 * COUNT, LANES), f32)], axis=0)
        ones = jnp.ones((8, 3 * LANES), bf16)
        parts = jnp.concatenate([p.astype(bf16) for p in split3(summed)], axis=1)
        part = lax.dot_general(ones, parts, (((1,), (1,)), ((), ())), preferred_element_type=f32)[0:1]
        message[step, 0] = part

        if step == 0:
            gather_all(step)
            pl.semaphore_wait(barrier, len(partners))
        for d in range(1, deep):
            column_copy(step, d).start()
        if step == 1:
            gather_all(step)
        send_ghosts(step)

        def own_quads(i, c):
            for v in range(4):
                own_quad(4 * i + v)
            return c

        def own_quad(q):
            tiles = []
            for u in range(4):
                t = 4 * q + u
                raw = own[pl.ds(pl.multiple_of(8 * t, 8), 8), :]
                tiles.append(raw)
                rows = jnp.concatenate(target_rows(raw), axis=0).astype(bf16)
                for quarter in range(4):
                    target_feat[4 * t + quarter, 32 * quarter : 32 * quarter + 32, :] = rows
                if step == 0:
                    source_str[t] = strength_rows(raw)
            source_quad(q, tiles)

        lax.fori_loop(0, TILES // 16, own_quads, 0)

        if step == 0:
            separation = (
                away_x.astype(f32),
                away_y.astype(f32),
                jnp.full((4, plane), (gz.astype(f32) + 0.5) * side - 0.5, f32),
            )
            for q, value in enumerate(derivatives(separation).values()):
                far_weights[4 * q : 4 * q + 4, :] = value

        else:
            for k in range(3):
                place(placer_start, start_flat, k, coords[k] + centre[k])
            for b in range(tall):
                for a in range(wide):
                    start_out[b, a] = start_flat[8 * (wide * b + a) : 8 * (wide * b + a) + 8, :]
            for d in range(1, tall):
                start_y_copy(d).start()
            for a in range(wide):
                start_mid[a, gy] = start_out[gy, a]

        all_column(step).wait_recv()
        total = message[step, 0]
        for d in range(1, deep):
            total = total + column_in[step, d - 1]
        message[step, 1] = total
        plane_in[step, rank] = total

        for d in others:
            plane_copy(step, d).start()

        for j in range(6):

            @pl.when(slots[j][2])
            def _():
                ghost_copy(step, j).wait_recv()

            axis, offset = slots[j][0], slots[j][1]
            moved = jnp.where(sub == axis, offset, 0.0)

            for q in range(GHOST_TILES // 4):
                tiles = []
                for u in range(4):
                    g = 4 * q + u
                    if step == 0:
                        raw = ghost_in[j, g]
                        source_str[TILES + j * GHOST_TILES + g] = strength_rows(raw)
                    elif u % 2 == 0:
                        raw = ghost_in_late[j, g // 2]
                    else:
                        raw = pltpu.roll(ghost_in_late[j, g // 2], 4, 0)
                    tiles.append(raw + moved)
                source_quad(TILES // 4 + j * (GHOST_TILES // 4) + q, tiles)

        def near(b, c):
            values = []
            for u in range(UNROLL):
                p = b * UNROLL + u
                t, s = targets[p], sources[p]
                gap = jnp.dot(source_feat[s >> 2], target_feat[4 * t + (s & 3)], preferred_element_type=f32)
                values.append(halves(lax.rsqrt(jnp.maximum(gap, core_sq))))
            for u in range(UNROLL):
                p = b * UNROLL + u
                pushed = source_str[sources[p]]
                pushed = jnp.concatenate([pushed, pushed], axis=1)
                both = jnp.concatenate(values[u], axis=0)
                contrib[pl.ds(pl.multiple_of(16 * p, 16), 16), :] = jnp.dot(
                    pushed, both, preferred_element_type=f32
                )
            return c

        lax.fori_loop(0, NPAIR // UNROLL // 2, near, 0)
        if step == 1:
            all_start_y().wait_recv()
            for d in range(1, wide):
                start_x_copy(d).start()
            start_in[gx] = start_mid[gx]
        lax.fori_loop(NPAIR // UNROLL // 2, NPAIR // UNROLL, near, 0)
        velocity = []
        for k in range(3):
            rows = contrib[pl.ds(3 + k, NPAIR, stride=16), :] + contrib[pl.ds(11 + k, NPAIR, stride=16), :]
            both = jnp.concatenate(halves(rows), axis=0)
            velocity.append(jnp.dot(chosen, both, preferred_element_type=f32))

        all_plane(step).wait_recv()
        for s in range(plane):
            gathered[s : s + 1, :] = plane_in[step, s]
        turned[...] = jnp.transpose(gathered[...])
        expansion = {}
        for m, inner in enumerate(TRIPLES):
            factor = (-1.0) ** sum(inner) / factorial(inner)
            source = jnp.where(is_far, turned[4 * m : 4 * m + 4, :] * factor, 0.0)
            for outer in TRIPLES:
                if sum(outer) + sum(inner) <= ORDER:
                    q = PLACE[tuple(a + b for a, b in zip(outer, inner))]
                    term = far_weights[4 * q : 4 * q + 4, :] * source
                    expansion[outer] = term if outer not in expansion else expansion[outer] + term
        for n, outer in enumerate(TRIPLES):
            value = jnp.sum(expansion[outer], axis=1, keepdims=True) * (1.0 / factorial(outer))
            local[4 * n : 4 * n + 4, :] = jnp.broadcast_to(value, (4, LANES))
        powers = monomials(coords)
        for n, outer in enumerate(TRIPLES):
            for k in range(3):
                term = jnp.broadcast_to(local[4 * n + k : 4 * n + k + 1, :], (TILES, LANES))
                if powers[outer] is not None:
                    term = term * powers[outer]
                velocity[k] = velocity[k] + term

        if step == 0:
            for k in range(3):
                own[pl.ds(k, TILES, stride=8), :] = coords[k] + time_step * velocity[k]

    for k in range(3):
        place(placer_speed, speed_out, k, velocity[k])

    for d in others:
        speed_copy(d).start()
    speed_in[speed_rows(rank), :] = speed_out[speed_rows(rank), :]
    all_start_x().wait_recv()
    for a in range(wide):
        for b in range(tall):
            start_flat[8 * (tall * a + b) : 8 * (tall * a + b) + 8, :] = start_in[a, b]
    for step in range(2):
        for j in range(6):

            @pl.when(slots[j][3])
            def _():
                ghost_copy(step, j).wait_send()

        all_column(step).wait_send()
        all_plane(step).wait_send()
    all_start_y().wait_send()
    all_start_x().wait_send()
    all_speed().wait_recv()
    for held, out in ((start_flat, out_start), (speed_in, out_speed)):
        for k in range(3):
            for r in range(CAP):
                out[k, pl.ds(r, plane, stride=CAP), :] = held[pl.ds(3 * r + k, plane, stride=8), :]
    all_speed().wait_send()


def finish(start, speed):
    moved = start + time_step * speed
    return moved.transpose(1, 0, 2), speed.transpose(1, 0, 2)


def per_device(offsets, strength, ghost_list, pair_targets, pair_sources, owners):
    sizes = tuple(lax.axis_size(axis) for axis in ("gx", "gy", "gz"))
    wide, tall, deep = sizes
    plane = wide * tall
    vmem = pl.BlockSpec(memory_space=pltpu.VMEM)
    smem = pl.BlockSpec(memory_space=pltpu.SMEM)
    hbm = pl.BlockSpec(memory_space=pltpu.HBM)
    shape = jax.ShapeDtypeStruct((3, plane * CAP, LANES), f32)
    dma = pltpu.SemaphoreType.DMA
    start, speed = pl.pallas_call(
        functools.partial(kernel, sizes),
        out_shape=(shape, shape),
        in_specs=[hbm, hbm, vmem, smem, vmem, smem, vmem],
        out_specs=(vmem, vmem),
        scratch_shapes=[
            pltpu.VMEM((3, SEG), f32),
            pltpu.VMEM((3, SEG), f32),
            pltpu.SemaphoreType.DMA((2,)),
            pltpu.VMEM((8 * TILES, LANES), f32),
            pltpu.VMEM((TILES // 2, 8, LANES), f32),
            pltpu.VMEM((GHOST_TILES, 8, LANES), f32),
            pltpu.VMEM((6, GHOST_TILES, 8, LANES), f32),
            pltpu.VMEM((GHOST_TILES // 2, 8, LANES), f32),
            pltpu.VMEM((6, GHOST_TILES // 2, 8, LANES), f32),
            pltpu.VMEM((4 * TILES, LANES, LANES), bf16),
            pltpu.VMEM((SOURCES // 4, LANES, LANES), bf16),
            pltpu.VMEM((SOURCES, 16, LANES), bf16),
            pltpu.VMEM((NPAIR * 16, LANES), f32),
            pltpu.VMEM((4 * COUNT * 8, LANES), f32),
            pltpu.VMEM((2, 2, 1, MESSAGE), f32),
            pltpu.VMEM((2, deep - 1, 1, MESSAGE), f32),
            pltpu.VMEM((2, plane, 1, MESSAGE), f32),
            pltpu.VMEM((plane, MESSAGE), f32),
            pltpu.VMEM((MESSAGE, plane), f32),
            pltpu.VMEM((4 * COUNT, LANES), f32),
            pltpu.VMEM((4 * COUNT, plane), f32),
            pltpu.VMEM((plane * 8, LANES), f32),
            pltpu.VMEM((tall, wide, 8, LANES), f32),
            pltpu.VMEM((wide, tall, 8, LANES), f32),
            pltpu.VMEM((wide, tall, 8, LANES), f32),
            pltpu.VMEM((plane * 8, LANES), f32),
            pltpu.VMEM((plane * 8, LANES), f32),
            dma((2, 6)),
            dma((2, 6)),
            dma((2,)),
            dma((2,)),
            dma((2,)),
            dma((2,)),
            dma((3,)),
            dma((3,)),
        ],
        compiler_params=pltpu.CompilerParams(
            collective_id=0, has_side_effects=True, vmem_limit_bytes=62 << 20
        ),
        name="dislocation_steps",
    )(offsets, strength, ghost_list, pair_targets, pair_targets, pair_sources, owners.reshape(1, TILES))
    return finish(start, speed)


def solution(mesh):
    return jax.shard_map(
        per_device,
        mesh=mesh,
        in_specs=(
            P(None, ("gx", "gy", "gz")),
            P(None, ("gx", "gy", "gz")),
            P(("gx", "gy", "gz")),
            P(("gx", "gy", "gz")),
            P(("gx", "gy", "gz")),
            P(("gx", "gy", "gz"), None),
        ),
        out_specs=(P(("gx", "gy", "gz"), None, None), P(("gx", "gy", "gz"), None, None)),
        check_vma=False,
    )
```

```python
import functools
import math

import jax
import jax.numpy as jnp
import numpy as np
from jax import lax
from jax.experimental import pallas as pl
from jax.experimental.pallas import tpu as pltpu
from jax.sharding import PartitionSpec as P

SEG = 4096
ORDER = 5
GHOST = 1536
NPAIR = 128
CAP = 2
LANES = 128
TILES = SEG // LANES
GHOST_TILES = GHOST // LANES
SOURCES = TILES + 6 * GHOST_TILES
UNROLL = 32

core_sq = 0.0025
time_step = 0.1
bf16 = jnp.bfloat16
f32 = jnp.float32
MESH = pl.DeviceIdType.MESH

TRIPLES = [
    (i, j, d - i - j)
    for d in range(ORDER + 1)
    for i in range(d, -1, -1)
    for j in range(d - i, -1, -1)
]
PLACE = {triple: at for at, triple in enumerate(TRIPLES)}
COUNT = len(TRIPLES)
MESSAGE = 256


def factorial(triple):
    return float(math.prod(math.factorial(e) for e in triple))


def lowered(triple, axis, by=1):
    out = list(triple)
    out[axis] -= by
    return tuple(out)


def monomials(coords):
    made = {}
    for triple in TRIPLES:
        if sum(triple) == 0:
            made[triple] = None
        else:
            axis = next(a for a in range(3) if triple[a])
            below = made[lowered(triple, axis)]
            made[triple] = coords[axis] if below is None else below * coords[axis]
    return made


def derivatives(separation):
    rx, ry, rz = separation
    inverse = 1.0 / (rx * rx + ry * ry + rz * rz + core_sq)
    taylor = {(0, 0, 0): lax.sqrt(inverse)}
    for triple in TRIPLES[1:]:
        n = sum(triple)
        first, second = None, None
        for axis in range(3):
            if triple[axis] >= 1:
                term = separation[axis] * taylor[lowered(triple, axis)]
                first = term if first is None else first + term
            if triple[axis] >= 2:
                term = taylor[lowered(triple, axis, 2)]
                second = term if second is None else second + term
        total = first * (-(2.0 * n - 1.0) / n)
        if second is not None:
            total = total - second * ((n - 1.0) / n)
        taylor[triple] = total * inverse
    return {t: v if factorial(t) == 1.0 else v * factorial(t) for t, v in taylor.items()}


def split3(value):
    high = value.astype(bf16).astype(f32)
    rest = value - high
    middle = rest.astype(bf16).astype(f32)
    return high, middle, rest - middle


def halves(value):
    high = value.astype(bf16)
    return high, (value - high.astype(f32)).astype(bf16)


def kernel(
    sizes,
    offsets_in, strength_in, ghost_list, targets, target_row, sources, owners,
    out_pos, out_vel,
    offsets, strength, input_done,
    own, paired, ghost_out, ghost_in, ghost_out_late, ghost_in_late, target_feat, source_feat, source_str, contrib, partial,
    message, column_in, plane_in, gathered, turned, local, far_weights,
    start_flat, start_out, start_mid, start_in, speed_out, speed_in,
    ghost_send, ghost_recv, column_send, column_recv, plane_send, plane_recv, block_send, block_recv,
):
    wide, tall, deep = sizes
    plane = wide * tall
    gx, gy, gz = lax.axis_index("gx"), lax.axis_index("gy"), lax.axis_index("gz")
    rank = gx * tall + gy
    shift = tall.bit_length() - 1
    side = 1.0 / deep
    sub = lax.broadcasted_iota(jnp.int32, (8, LANES), 0)

    def along(d):
        return (gx, gy, (gz + d) & (deep - 1))

    def across(d):
        return ((gx + d[0]) & (wide - 1), (gy + d[1]) & (tall - 1), gz)

    def hops(d):
        return min(d[0], wide - d[0]) + min(d[1], tall - d[1])

    others = [(x, y) for x in range(wide) for y in range(tall) if x + y > 0]
    others.sort(key=hops, reverse=True)

    load_offsets = pltpu.make_async_copy(offsets_in, offsets, input_done.at[0])
    load_strength = pltpu.make_async_copy(strength_in, strength, input_done.at[1])
    load_offsets.start()
    load_strength.start()

    def along_y(d):
        return (gx, (gy + d) & (tall - 1), gz)

    def along_x(d):
        return ((gx + d) & (wide - 1), gy, gz)

    barrier = pltpu.get_barrier_semaphore()

    partners = [across(d) for d in others] + [along(d) for d in range(1, deep)]
    for partner in partners:
        pl.semaphore_signal(barrier, inc=1, device_id=partner, device_id_type=MESH)

    position = (gx, gy, gz)
    slots = []
    for axis, count in enumerate((wide, tall, deep)):
        at = position[axis]
        up = tuple(p + 1 if i == axis else p for i, p in enumerate(position))
        down = tuple(p - 1 if i == axis else p for i, p in enumerate(position))
        step = side if axis == 2 else 1.0
        slots.append((axis, -step, at > 0, at < count - 1, up))
        slots.append((axis, step, at < count - 1, at > 0, down))

    scale = jnp.where(lax.broadcasted_iota(jnp.int32, (3, LANES), 0) == 2, side, 1.0)
    own[...] = jnp.zeros_like(own)
    target_feat[...] = jnp.zeros_like(target_feat)
    start_flat[...] = jnp.zeros_like(start_flat)
    speed_out[...] = jnp.zeros_like(speed_out)
    load_offsets.wait()
    load_strength.wait()
    for t in range(TILES):
        lanes = slice(t * LANES, (t + 1) * LANES)
        own[8 * t : 8 * t + 3, :] = (offsets[:, lanes] - 0.5) * scale
        own[8 * t + 3 : 8 * t + 6, :] = strength[:, lanes]

    def dense(row):
        return own[pl.ds(row, TILES, stride=8), :]

    dense_strength = [dense(3 + k) for k in range(3)]

    lane = lax.broadcasted_iota(jnp.int32, (4, plane), 1)
    source_x, source_y = lane >> shift, lane & (tall - 1)
    away_x, away_y = gx - source_x, gy - source_y
    is_far = jnp.maximum(jnp.abs(away_x), jnp.abs(away_y)) >= 3

    rows_i = lax.broadcasted_iota(jnp.int32, (TILES, TILES), 0)
    cols_i = lax.broadcasted_iota(jnp.int32, (TILES, TILES), 1)
    row_f = owners[...].astype(f32)
    column_f = jnp.sum(jnp.where(rows_i == cols_i, row_f, 0.0), axis=1, keepdims=True)
    earlier = jnp.where((column_f == row_f) & (rows_i < cols_i), 1.0, 0.0)
    nth_f = jnp.sum(earlier, axis=0, keepdims=True) * plane
    slot_rows = lax.broadcasted_iota(jnp.int32, (CAP * plane, TILES), 0).astype(f32)

    def placer_of(order_f):
        placer = jnp.where(slot_rows == nth_f + order_f, 1.0, 0.0).astype(bf16)
        return jnp.concatenate([placer, placer, placer], axis=1)

    row_i = owners[...]
    placer_start = placer_of(((row_i & (tall - 1)) * wide + (row_i >> shift)).astype(f32))
    placer_speed = placer_of(row_f)

    def place(placer, out, k, field):
        parts = jnp.concatenate([p.astype(bf16) for p in split3(field)], axis=0)
        placed = jnp.dot(placer, parts, preferred_element_type=f32)
        for r in range(CAP):
            out[pl.ds(3 * r + k, plane, stride=8), :] = placed[r * plane : (r + 1) * plane]

    def remote(src, dst, send_sem, recv_sem, device):
        return pltpu.make_async_remote_copy(
            src_ref=src,
            dst_ref=dst,
            send_sem=send_sem,
            recv_sem=recv_sem,
            device_id=device,
            device_id_type=MESH,
        )

    def speed_rows(o):
        return pl.ds(pl.multiple_of(8 * o, 8), 3 * CAP)

    def speed_copy(d):
        target = across(d)
        other = target[0] * tall + target[1]
        return remote(
            speed_out.at[speed_rows(other)], speed_in.at[speed_rows(rank)], block_send.at[0], block_recv.at[0], target
        )

    def all_speed():
        rows = pl.ds(0, (plane - 1) * 3 * CAP)
        return remote(speed_out.at[rows], speed_in.at[rows], block_send.at[0], block_recv.at[0], across(others[0]))

    def start_y_copy(d):
        target = along_y(d)
        return remote(
            start_out.at[target[1], :, pl.ds(0, 3 * CAP)], start_mid.at[:, gy, pl.ds(0, 3 * CAP)], block_send.at[1], block_recv.at[1], target
        )

    def all_start_y():
        part = start_mid.at[:, pl.ds(0, tall - 1), pl.ds(0, 3 * CAP)]
        return remote(part, part, block_send.at[1], block_recv.at[1], along_y(1))

    def start_x_copy(d):
        target = along_x(d)
        return remote(
            start_mid.at[target[0], :, pl.ds(0, 3 * CAP)], start_in.at[gx, :, pl.ds(0, 3 * CAP)], block_send.at[2], block_recv.at[2], target
        )

    def all_start_x():
        part = start_in.at[pl.ds(0, wide - 1), :, pl.ds(0, 3 * CAP)]
        return remote(part, part, block_send.at[2], block_recv.at[2], along_x(1))

    def ghost_copy(step, j):
        return pltpu.make_async_remote_copy(
            src_ref=ghost_out if step == 0 else ghost_out_late,
            dst_ref=ghost_in.at[j] if step == 0 else ghost_in_late.at[j],
            send_sem=ghost_send.at[step, j],
            recv_sem=ghost_recv.at[step, j],
            device_id=slots[j][4],
            device_id_type=MESH,
        )

    def column_copy(step, d):
        return pltpu.make_async_remote_copy(
            src_ref=message.at[step, 0],
            dst_ref=column_in.at[step, d - 1],
            send_sem=column_send.at[step],
            recv_sem=column_recv.at[step],
            device_id=along(d),
            device_id_type=MESH,
        )

    def all_column(step):
        return pltpu.make_async_remote_copy(
            src_ref=column_in.at[step],
            dst_ref=column_in.at[step],
            send_sem=column_send.at[step],
            recv_sem=column_recv.at[step],
            device_id=along(1),
            device_id_type=MESH,
        )

    def plane_copy(step, d):
        return remote(
            message.at[step, 1], plane_in.at[step, rank], plane_send.at[step], plane_recv.at[step], across(d)
        )

    def all_plane(step):
        rows = plane_in.at[step, pl.ds(0, plane - 1)]
        return remote(rows, rows, plane_send.at[step], plane_recv.at[step], across(others[0]))

    for j in range(6):

        @pl.when(jnp.logical_not(slots[j][2]))
        def _():
            ghost_in[j] = jnp.zeros((GHOST_TILES, 8, LANES), f32)
            ghost_in_late[j] = jnp.zeros((GHOST_TILES // 2, 8, LANES), f32)

    centre = (gx.astype(f32) + 0.5, gy.astype(f32) + 0.5, (gz.astype(f32) + 0.5) * side)
    zeros8 = jnp.zeros((8, LANES), f32)

    def squares(raw):
        return jnp.sum(jnp.where(sub < 3, raw * raw, 0.0), axis=0, keepdims=True)

    def source_rows(raw):
        mixed = jnp.where(sub < 3, raw, jnp.where(sub < 6, pltpu.roll(raw, 3, 0), 1.0))
        value = jnp.where(sub == 6, squares(raw), mixed)
        high, middle, low = split3(value)
        return [
            high,
            jnp.where(sub == 7, high, middle),
            jnp.where((sub < 3) | (sub == 6), low, high),
            zeros8,
        ]

    def target_rows(raw):
        mixed = jnp.where(sub < 3, -2.0 * raw, jnp.where(sub < 6, -2.0 * pltpu.roll(raw, 3, 0), 1.0))
        value = jnp.where(sub == 7, squares(raw) + core_sq, mixed)
        high, middle, low = split3(value)
        second = (sub >= 3) & (sub < 6)
        last = second | (sub == 7)
        return [
            jnp.where(second, middle, high),
            jnp.where(last, middle, high),
            jnp.where(last, low, high),
            zeros8,
        ]

    def strength_rows(raw):
        high = raw.astype(bf16).astype(f32)
        return jnp.concatenate([high, raw - high], axis=0).astype(bf16)

    def source_quad(quad, tiles):
        rows = [row for raw in tiles for row in source_rows(raw)]
        source_feat[quad] = jnp.transpose(jnp.concatenate(rows, axis=0)).astype(bf16)

    chosen = (lax.broadcasted_iota(jnp.int32, (TILES, NPAIR), 0) == target_row[...].reshape(1, NPAIR))
    chosen = jnp.where(chosen, 1.0, 0.0).astype(bf16)
    chosen = jnp.concatenate([chosen, chosen], axis=1)

    def ghost_index(g):
        index = ghost_list[pl.ds(pl.multiple_of(g * LANES, LANES), LANES)].reshape(1, LANES)
        return jnp.broadcast_to(index & (LANES - 1), (8, LANES)), jnp.broadcast_to(index >> 7, (8, LANES))

    def take(tile, low):
        return jnp.take_along_axis(tile, low, axis=1, mode="promise_in_bounds")

    def gather_all(step):
        def whole(g, c):
            low, high = ghost_index(g)
            found = zeros8
            for t in range(TILES):
                found = jnp.where(high == t, take(own[8 * t : 8 * t + 8, :], low), found)
            ghost_out[g] = found
            return c

        def pair(g, c):
            both = []
            for u in range(2):
                low, high = ghost_index(2 * g + u)
                high = high - (sub >> 2)
                found = zeros8
                for t in range(TILES // 2):
                    found = jnp.where(high == 2 * t, take(paired[t], low), found)
                both.append(found + pltpu.roll(found, 4, 0))
            ghost_out_late[g] = jnp.where(sub < 4, both[0], both[1])
            return c

        if step == 0:
            lax.fori_loop(0, GHOST_TILES, whole, 0)
        else:
            for t in range(TILES // 2):
                first, second = own[16 * t : 16 * t + 8, :], own[16 * t + 8 : 16 * t + 16, :]
                paired[t] = jnp.where(sub < 4, first, pltpu.roll(second, 4, 0))
            lax.fori_loop(0, GHOST_TILES // 2, pair, 0)

    def send_ghosts(step):
        for j in range(6):

            @pl.when(slots[j][3])
            def _():
                ghost_copy(step, j).start()

    velocity = None
    for step in range(2):

        coords = [dense(k) for k in range(3)]
        centred = [coords[0], coords[1], coords[2] + ((gz.astype(f32) + 0.5) * side - 0.5)]
        powers = monomials(centred)
        for m, triple in enumerate(TRIPLES):
            for k in range(3):
                term = dense_strength[k]
                if powers[triple] is not None:
                    term = term * powers[triple]
                folded = functools.reduce(lambda a, b: a + b, [term[8 * i : 8 * i + 8] for i in range(TILES // 8)])
                partial[8 * (4 * m + k) : 8 * (4 * m + k) + 8, :] = folded
            if step == 0:
                partial[8 * (4 * m + 3) : 8 * (4 * m + 3) + 8, :] = zeros8
        summed = None
        for i in range(8):
            rows = partial[pl.ds(i, 4 * COUNT, stride=8), :]
            summed = rows if summed is None else summed + rows
        summed = jnp.concatenate([summed, jnp.zeros((MESSAGE - 4 * COUNT, LANES), f32)], axis=0)
        ones = jnp.ones((8, 3 * LANES), bf16)
        parts = jnp.concatenate([p.astype(bf16) for p in split3(summed)], axis=1)
        part = lax.dot_general(ones, parts, (((1,), (1,)), ((), ())), preferred_element_type=f32)[0:1]
        message[step, 0] = part

        if step == 0:
            gather_all(step)
            pl.semaphore_wait(barrier, len(partners))
        for d in range(1, deep):
            column_copy(step, d).start()
        if step == 1:
            gather_all(step)
        send_ghosts(step)

        def own_quads(i, c):
            for v in range(4):
                own_quad(4 * i + v)
            return c

        def own_quad(q):
            tiles = []
            for u in range(4):
                t = 4 * q + u
                raw = own[pl.ds(pl.multiple_of(8 * t, 8), 8), :]
                tiles.append(raw)
                rows = jnp.concatenate(target_rows(raw), axis=0).astype(bf16)
                for quarter in range(4):
                    target_feat[4 * t + quarter, 32 * quarter : 32 * quarter + 32, :] = rows
                if step == 0:
                    source_str[t] = strength_rows(raw)
            source_quad(q, tiles)

        lax.fori_loop(0, TILES // 16, own_quads, 0)

        if step == 0:
            separation = (
                away_x.astype(f32),
                away_y.astype(f32),
                jnp.full((4, plane), (gz.astype(f32) + 0.5) * side - 0.5, f32),
            )
            for q, value in enumerate(derivatives(separation).values()):
                far_weights[4 * q : 4 * q + 4, :] = value

        else:
            for k in range(3):
                place(placer_start, start_flat, k, coords[k] + centre[k])
            for b in range(tall):
                for a in range(wide):
                    start_out[b, a] = start_flat[8 * (wide * b + a) : 8 * (wide * b + a) + 8, :]
            for d in range(1, tall):
                start_y_copy(d).start()
            for a in range(wide):
                start_mid[a, gy] = start_out[gy, a]

        all_column(step).wait_recv()
        total = message[step, 0]
        for d in range(1, deep):
            total = total + column_in[step, d - 1]
        message[step, 1] = total
        plane_in[step, rank] = total

        for d in others:
            plane_copy(step, d).start()

        for j in range(6):

            @pl.when(slots[j][2])
            def _():
                ghost_copy(step, j).wait_recv()

            axis, offset = slots[j][0], slots[j][1]
            moved = jnp.where(sub == axis, offset, 0.0)

            for q in range(GHOST_TILES // 4):
                tiles = []
                for u in range(4):
                    g = 4 * q + u
                    if step == 0:
                        raw = ghost_in[j, g]
                        source_str[TILES + j * GHOST_TILES + g] = strength_rows(raw)
                    elif u % 2 == 0:
                        raw = ghost_in_late[j, g // 2]
                    else:
                        raw = pltpu.roll(ghost_in_late[j, g // 2], 4, 0)
                    tiles.append(raw + moved)
                source_quad(TILES // 4 + j * (GHOST_TILES // 4) + q, tiles)

        def near(b, c):
            values = []
            for u in range(UNROLL):
                p = b * UNROLL + u
                t, s = targets[p], sources[p]
                gap = jnp.dot(source_feat[s >> 2], target_feat[4 * t + (s & 3)], preferred_element_type=f32)
                values.append(halves(lax.rsqrt(jnp.maximum(gap, core_sq))))
            for u in range(UNROLL):
                p = b * UNROLL + u
                pushed = source_str[sources[p]]
                pushed = jnp.concatenate([pushed, pushed], axis=1)
                both = jnp.concatenate(values[u], axis=0)
                contrib[pl.ds(pl.multiple_of(16 * p, 16), 16), :] = jnp.dot(
                    pushed, both, preferred_element_type=f32
                )
            return c

        lax.fori_loop(0, NPAIR // UNROLL // 2, near, 0)
        if step == 1:
            all_start_y().wait_recv()
            for d in range(1, wide):
                start_x_copy(d).start()
            start_in[gx] = start_mid[gx]
        lax.fori_loop(NPAIR // UNROLL // 2, NPAIR // UNROLL, near, 0)
        velocity = []
        for k in range(3):
            rows = contrib[pl.ds(3 + k, NPAIR, stride=16), :] + contrib[pl.ds(11 + k, NPAIR, stride=16), :]
            both = jnp.concatenate(halves(rows), axis=0)
            velocity.append(jnp.dot(chosen, both, preferred_element_type=f32))

        all_plane(step).wait_recv()
        for s in range(plane):
            gathered[s : s + 1, :] = plane_in[step, s]
        turned[...] = jnp.transpose(gathered[...])
        expansion = {}
        for m, inner in enumerate(TRIPLES):
            factor = (-1.0) ** sum(inner) / factorial(inner)
            source = jnp.where(is_far, turned[4 * m : 4 * m + 4, :] * factor, 0.0)
            for outer in TRIPLES:
                if sum(outer) + sum(inner) <= ORDER:
                    q = PLACE[tuple(a + b for a, b in zip(outer, inner))]
                    term = far_weights[4 * q : 4 * q + 4, :] * source
                    expansion[outer] = term if outer not in expansion else expansion[outer] + term
        for n, outer in enumerate(TRIPLES):
            value = jnp.sum(expansion[outer], axis=1, keepdims=True) * (1.0 / factorial(outer))
            local[4 * n : 4 * n + 4, :] = jnp.broadcast_to(value, (4, LANES))
        powers = monomials(coords)
        for n, outer in enumerate(TRIPLES):
            for k in range(3):
                term = jnp.broadcast_to(local[4 * n + k : 4 * n + k + 1, :], (TILES, LANES))
                if powers[outer] is not None:
                    term = term * powers[outer]
                velocity[k] = velocity[k] + term

        if step == 0:
            for k in range(3):
                own[pl.ds(k, TILES, stride=8), :] = coords[k] + time_step * velocity[k]

    for k in range(3):
        place(placer_speed, speed_out, k, velocity[k])

    for d in others:
        speed_copy(d).start()
    speed_in[speed_rows(rank), :] = speed_out[speed_rows(rank), :]
    all_start_x().wait_recv()
    for a in range(wide):
        for b in range(tall):
            start_flat[8 * (tall * a + b) : 8 * (tall * a + b) + 8, :] = start_in[a, b]
    for step in range(2):
        for j in range(6):

            @pl.when(slots[j][3])
            def _():
                ghost_copy(step, j).wait_send()

        all_column(step).wait_send()
        all_plane(step).wait_send()
    all_start_y().wait_send()
    all_start_x().wait_send()
    all_speed().wait_recv()
    for k in range(3):
        for r in range(CAP):
            held = pl.ds(3 * r + k, plane, stride=8)
            slot = pl.ds(r, plane, stride=CAP)
            out_vel[k, slot, :] = speed_in[held, :]
            out_pos[k, slot, :] = start_flat[held, :] + time_step * speed_in[held, :]
    all_speed().wait_send()


def hand_on(pos_in, vel_in, pos_out, vel_out, done):
    first = pltpu.make_async_copy(pos_in, pos_out, done.at[0])
    second = pltpu.make_async_copy(vel_in, vel_out, done.at[1])
    first.start()
    second.start()
    first.wait()
    second.wait()


def finish(positions, velocity):
    hbm = pl.BlockSpec(memory_space=pltpu.HBM)
    vmem = pl.BlockSpec(memory_space=pltpu.VMEM)
    positions, velocity = pl.pallas_call(
        hand_on,
        out_shape=tuple(jax.ShapeDtypeStruct(a.shape, a.dtype) for a in (positions, velocity)),
        in_specs=[vmem, vmem],
        out_specs=(hbm, hbm),
        scratch_shapes=[pltpu.SemaphoreType.DMA((2,))],
        name="hand_on",
    )(positions, velocity)
    return positions.transpose(1, 0, 2), velocity.transpose(1, 0, 2)


def per_device(offsets, strength, ghost_list, pair_targets, pair_sources, owners):
    sizes = tuple(lax.axis_size(axis) for axis in ("gx", "gy", "gz"))
    wide, tall, deep = sizes
    plane = wide * tall
    vmem = pl.BlockSpec(memory_space=pltpu.VMEM)
    smem = pl.BlockSpec(memory_space=pltpu.SMEM)
    hbm = pl.BlockSpec(memory_space=pltpu.HBM)
    shape = jax.ShapeDtypeStruct((3, plane * CAP, LANES), f32)
    dma = pltpu.SemaphoreType.DMA
    positions, velocity = pl.pallas_call(
        functools.partial(kernel, sizes),
        out_shape=(shape, shape),
        in_specs=[hbm, hbm, vmem, smem, vmem, smem, vmem],
        out_specs=(vmem, vmem),
        scratch_shapes=[
            pltpu.VMEM((3, SEG), f32),
            pltpu.VMEM((3, SEG), f32),
            pltpu.SemaphoreType.DMA((2,)),
            pltpu.VMEM((8 * TILES, LANES), f32),
            pltpu.VMEM((TILES // 2, 8, LANES), f32),
            pltpu.VMEM((GHOST_TILES, 8, LANES), f32),
            pltpu.VMEM((6, GHOST_TILES, 8, LANES), f32),
            pltpu.VMEM((GHOST_TILES // 2, 8, LANES), f32),
            pltpu.VMEM((6, GHOST_TILES // 2, 8, LANES), f32),
            pltpu.VMEM((4 * TILES, LANES, LANES), bf16),
            pltpu.VMEM((SOURCES // 4, LANES, LANES), bf16),
            pltpu.VMEM((SOURCES, 16, LANES), bf16),
            pltpu.VMEM((NPAIR * 16, LANES), f32),
            pltpu.VMEM((4 * COUNT * 8, LANES), f32),
            pltpu.VMEM((2, 2, 1, MESSAGE), f32),
            pltpu.VMEM((2, deep - 1, 1, MESSAGE), f32),
            pltpu.VMEM((2, plane, 1, MESSAGE), f32),
            pltpu.VMEM((plane, MESSAGE), f32),
            pltpu.VMEM((MESSAGE, plane), f32),
            pltpu.VMEM((4 * COUNT, LANES), f32),
            pltpu.VMEM((4 * COUNT, plane), f32),
            pltpu.VMEM((plane * 8, LANES), f32),
            pltpu.VMEM((tall, wide, 8, LANES), f32),
            pltpu.VMEM((wide, tall, 8, LANES), f32),
            pltpu.VMEM((wide, tall, 8, LANES), f32),
            pltpu.VMEM((plane * 8, LANES), f32),
            pltpu.VMEM((plane * 8, LANES), f32),
            dma((2, 6)),
            dma((2, 6)),
            dma((2,)),
            dma((2,)),
            dma((2,)),
            dma((2,)),
            dma((3,)),
            dma((3,)),
        ],
        compiler_params=pltpu.CompilerParams(
            collective_id=0, has_side_effects=True, vmem_limit_bytes=62 << 20
        ),
        name="dislocation_steps",
    )(offsets, strength, ghost_list, pair_targets, pair_targets, pair_sources, owners.reshape(1, TILES))
    return finish(positions, velocity)


def solution(mesh):
    return jax.shard_map(
        per_device,
        mesh=mesh,
        in_specs=(
            P(None, ("gx", "gy", "gz")),
            P(None, ("gx", "gy", "gz")),
            P(("gx", "gy", "gz")),
            P(("gx", "gy", "gz")),
            P(("gx", "gy", "gz")),
            P(("gx", "gy", "gz"), None),
        ),
        out_specs=(P(("gx", "gy", "gz"), None, None), P(("gx", "gy", "gz"), None, None)),
        check_vma=False,
    )
```

```python
import functools
import math

import jax
import jax.numpy as jnp
import numpy as np
from jax import lax
from jax.experimental import pallas as pl
from jax.experimental.pallas import tpu as pltpu
from jax.sharding import PartitionSpec as P

SEG = 4096
ORDER = 5
GHOST = 1536
NPAIR = 128
CAP = 2
LANES = 128
TILES = SEG // LANES
GHOST_TILES = GHOST // LANES
SOURCES = TILES + 6 * GHOST_TILES
UNROLL = 32

core_sq = 0.0025
time_step = 0.1
bf16 = jnp.bfloat16
f32 = jnp.float32
MESH = pl.DeviceIdType.MESH

TRIPLES = [
    (i, j, d - i - j)
    for d in range(ORDER + 1)
    for i in range(d, -1, -1)
    for j in range(d - i, -1, -1)
]
PLACE = {triple: at for at, triple in enumerate(TRIPLES)}
COUNT = len(TRIPLES)
MESSAGE = 256


def factorial(triple):
    return float(math.prod(math.factorial(e) for e in triple))


def lowered(triple, axis, by=1):
    out = list(triple)
    out[axis] -= by
    return tuple(out)


def monomials(coords):
    made = {}
    for triple in TRIPLES:
        if sum(triple) == 0:
            made[triple] = None
        else:
            axis = next(a for a in range(3) if triple[a])
            below = made[lowered(triple, axis)]
            made[triple] = coords[axis] if below is None else below * coords[axis]
    return made


def derivatives(separation):
    rx, ry, rz = separation
    inverse = 1.0 / (rx * rx + ry * ry + rz * rz + core_sq)
    taylor = {(0, 0, 0): lax.sqrt(inverse)}
    for triple in TRIPLES[1:]:
        n = sum(triple)
        first, second = None, None
        for axis in range(3):
            if triple[axis] >= 1:
                term = separation[axis] * taylor[lowered(triple, axis)]
                first = term if first is None else first + term
            if triple[axis] >= 2:
                term = taylor[lowered(triple, axis, 2)]
                second = term if second is None else second + term
        total = first * (-(2.0 * n - 1.0) / n)
        if second is not None:
            total = total - second * ((n - 1.0) / n)
        taylor[triple] = total * inverse
    return {t: v if factorial(t) == 1.0 else v * factorial(t) for t, v in taylor.items()}


def split3(value):
    high = value.astype(bf16).astype(f32)
    rest = value - high
    middle = rest.astype(bf16).astype(f32)
    return high, middle, rest - middle


def halves(value):
    high = value.astype(bf16)
    return high, (value - high.astype(f32)).astype(bf16)


def kernel(
    sizes,
    offsets_in, strength_in, ghost_list, targets, target_row, sources, owners,
    out_pos, out_vel,
    offsets, strength, input_done,
    own, paired, ghost_out, ghost_in, ghost_out_late, ghost_in_late, target_feat, source_feat, source_str, contrib, partial,
    message, column_in, plane_in, gathered, turned, local, far_weights,
    start_flat, start_out, start_mid, start_in, speed_out, speed_in,
    ghost_send, ghost_recv, column_send, column_recv, plane_send, plane_recv, block_send, block_recv,
):
    wide, tall, deep = sizes
    plane = wide * tall
    gx, gy, gz = lax.axis_index("gx"), lax.axis_index("gy"), lax.axis_index("gz")
    rank = gx * tall + gy
    shift = tall.bit_length() - 1
    side = 1.0 / deep
    sub = lax.broadcasted_iota(jnp.int32, (8, LANES), 0)

    def along(d):
        return (gx, gy, (gz + d) & (deep - 1))

    def across(d):
        return ((gx + d[0]) & (wide - 1), (gy + d[1]) & (tall - 1), gz)

    def hops(d):
        return min(d[0], wide - d[0]) + min(d[1], tall - d[1])

    others = [(x, y) for x in range(wide) for y in range(tall) if x + y > 0]
    others.sort(key=hops, reverse=True)

    load_offsets = pltpu.make_async_copy(offsets_in, offsets, input_done.at[0])
    load_strength = pltpu.make_async_copy(strength_in, strength, input_done.at[1])
    load_offsets.start()
    load_strength.start()

    def along_y(d):
        return (gx, (gy + d) & (tall - 1), gz)

    def along_x(d):
        return ((gx + d) & (wide - 1), gy, gz)

    barrier = pltpu.get_barrier_semaphore()

    partners = [across(d) for d in others] + [along(d) for d in range(1, deep)]
    for partner in partners:
        pl.semaphore_signal(barrier, inc=1, device_id=partner, device_id_type=MESH)

    position = (gx, gy, gz)
    slots = []
    for axis, count in enumerate((wide, tall, deep)):
        at = position[axis]
        up = tuple(p + 1 if i == axis else p for i, p in enumerate(position))
        down = tuple(p - 1 if i == axis else p for i, p in enumerate(position))
        step = side if axis == 2 else 1.0
        slots.append((axis, -step, at > 0, at < count - 1, up))
        slots.append((axis, step, at < count - 1, at > 0, down))

    scale = jnp.where(lax.broadcasted_iota(jnp.int32, (3, LANES), 0) == 2, side, 1.0)
    own[...] = jnp.zeros_like(own)
    start_flat[...] = jnp.zeros_like(start_flat)
    speed_out[...] = jnp.zeros_like(speed_out)
    load_offsets.wait()
    load_strength.wait()
    for t in range(TILES):
        lanes = slice(t * LANES, (t + 1) * LANES)
        own[8 * t : 8 * t + 3, :] = (offsets[:, lanes] - 0.5) * scale
        own[8 * t + 3 : 8 * t + 6, :] = strength[:, lanes]

    def dense(row):
        return own[pl.ds(row, TILES, stride=8), :]

    dense_strength = [dense(3 + k) for k in range(3)]

    lane = lax.broadcasted_iota(jnp.int32, (4, plane), 1)
    source_x, source_y = lane >> shift, lane & (tall - 1)
    away_x, away_y = gx - source_x, gy - source_y
    is_far = jnp.maximum(jnp.abs(away_x), jnp.abs(away_y)) >= 3

    rows_i = lax.broadcasted_iota(jnp.int32, (TILES, TILES), 0)
    cols_i = lax.broadcasted_iota(jnp.int32, (TILES, TILES), 1)
    row_f = owners[...].astype(f32)
    column_f = jnp.sum(jnp.where(rows_i == cols_i, row_f, 0.0), axis=1, keepdims=True)
    earlier = jnp.where((column_f == row_f) & (rows_i < cols_i), 1.0, 0.0)
    nth_f = jnp.sum(earlier, axis=0, keepdims=True) * plane
    slot_rows = lax.broadcasted_iota(jnp.int32, (CAP * plane, TILES), 0).astype(f32)

    def placer_of(order_f):
        placer = jnp.where(slot_rows == nth_f + order_f, 1.0, 0.0).astype(bf16)
        return jnp.concatenate([placer, placer, placer], axis=1)

    row_i = owners[...]
    placer_start = placer_of(((row_i & (tall - 1)) * wide + (row_i >> shift)).astype(f32))
    placer_speed = placer_of(row_f)

    def place(placer, out, k, field):
        parts = jnp.concatenate([p.astype(bf16) for p in split3(field)], axis=0)
        placed = jnp.dot(placer, parts, preferred_element_type=f32)
        for r in range(CAP):
            out[pl.ds(3 * r + k, plane, stride=8), :] = placed[r * plane : (r + 1) * plane]

    def remote(src, dst, send_sem, recv_sem, device):
        return pltpu.make_async_remote_copy(
            src_ref=src,
            dst_ref=dst,
            send_sem=send_sem,
            recv_sem=recv_sem,
            device_id=device,
            device_id_type=MESH,
        )

    def speed_rows(o):
        return pl.ds(pl.multiple_of(8 * o, 8), 3 * CAP)

    def speed_copy(d):
        target = across(d)
        other = target[0] * tall + target[1]
        return remote(
            speed_out.at[speed_rows(other)], speed_in.at[speed_rows(rank)], block_send.at[0], block_recv.at[0], target
        )

    def all_speed():
        rows = pl.ds(0, (plane - 1) * 3 * CAP)
        return remote(speed_out.at[rows], speed_in.at[rows], block_send.at[0], block_recv.at[0], across(others[0]))

    def start_y_copy(d):
        target = along_y(d)
        return remote(
            start_out.at[target[1], :, pl.ds(0, 3 * CAP)], start_mid.at[:, gy, pl.ds(0, 3 * CAP)], block_send.at[1], block_recv.at[1], target
        )

    def all_start_y():
        part = start_mid.at[:, pl.ds(0, tall - 1), pl.ds(0, 3 * CAP)]
        return remote(part, part, block_send.at[1], block_recv.at[1], along_y(1))

    def start_x_copy(d):
        target = along_x(d)
        return remote(
            start_mid.at[target[0], :, pl.ds(0, 3 * CAP)], start_in.at[gx, :, pl.ds(0, 3 * CAP)], block_send.at[2], block_recv.at[2], target
        )

    def all_start_x():
        part = start_in.at[pl.ds(0, wide - 1), :, pl.ds(0, 3 * CAP)]
        return remote(part, part, block_send.at[2], block_recv.at[2], along_x(1))

    def ghost_copy(step, j):
        return pltpu.make_async_remote_copy(
            src_ref=ghost_out if step == 0 else ghost_out_late,
            dst_ref=ghost_in.at[j] if step == 0 else ghost_in_late.at[j],
            send_sem=ghost_send.at[step, j],
            recv_sem=ghost_recv.at[step, j],
            device_id=slots[j][4],
            device_id_type=MESH,
        )

    def column_copy(step, d):
        return pltpu.make_async_remote_copy(
            src_ref=message.at[step, 0],
            dst_ref=column_in.at[step, d - 1],
            send_sem=column_send.at[step],
            recv_sem=column_recv.at[step],
            device_id=along(d),
            device_id_type=MESH,
        )

    def all_column(step):
        return pltpu.make_async_remote_copy(
            src_ref=column_in.at[step],
            dst_ref=column_in.at[step],
            send_sem=column_send.at[step],
            recv_sem=column_recv.at[step],
            device_id=along(1),
            device_id_type=MESH,
        )

    def plane_copy(step, d):
        return remote(
            message.at[step, 1], plane_in.at[step, rank], plane_send.at[step], plane_recv.at[step], across(d)
        )

    def all_plane(step):
        rows = plane_in.at[step, pl.ds(0, plane - 1)]
        return remote(rows, rows, plane_send.at[step], plane_recv.at[step], across(others[0]))

    for j in range(6):

        @pl.when(jnp.logical_not(slots[j][2]))
        def _():
            ghost_in[j] = jnp.zeros((GHOST_TILES, 8, LANES), f32)
            ghost_in_late[j] = jnp.zeros((GHOST_TILES // 2, 8, LANES), f32)

    centre = (gx.astype(f32) + 0.5, gy.astype(f32) + 0.5, (gz.astype(f32) + 0.5) * side)
    zeros8 = jnp.zeros((8, LANES), f32)

    def squares(raw):
        return jnp.sum(jnp.where(sub < 3, raw * raw, 0.0), axis=0, keepdims=True)

    def source_rows(raw):
        mixed = jnp.where(sub < 3, raw, jnp.where(sub < 6, pltpu.roll(raw, 3, 0), 1.0))
        value = jnp.where(sub == 6, squares(raw), mixed)
        high, middle, low = split3(value)
        return [
            high,
            jnp.where(sub == 7, high, middle),
            jnp.where((sub < 3) | (sub == 6), low, high),
            zeros8,
        ]

    def target_rows(raw):
        mixed = jnp.where(sub < 3, -2.0 * raw, jnp.where(sub < 6, -2.0 * pltpu.roll(raw, 3, 0), 1.0))
        value = jnp.where(sub == 7, squares(raw) + core_sq, mixed)
        high, middle, low = split3(value)
        second = (sub >= 3) & (sub < 6)
        last = second | (sub == 7)
        return [
            jnp.where(second, middle, high),
            jnp.where(last, middle, high),
            jnp.where(last, low, high),
            zeros8,
        ]

    def strength_rows(raw):
        high = raw.astype(bf16).astype(f32)
        return jnp.concatenate([high, raw - high], axis=0).astype(bf16)

    def source_quad(quad, tiles):
        rows = [row for raw in tiles for row in source_rows(raw)]
        source_feat[quad] = jnp.transpose(jnp.concatenate(rows, axis=0)).astype(bf16)

    chosen = (lax.broadcasted_iota(jnp.int32, (TILES, NPAIR), 0) == target_row[...].reshape(1, NPAIR))
    chosen = jnp.where(chosen, 1.0, 0.0).astype(bf16)
    chosen = jnp.concatenate([chosen, chosen], axis=1)

    def ghost_index(g):
        index = ghost_list[pl.ds(pl.multiple_of(g * LANES, LANES), LANES)].reshape(1, LANES)
        return jnp.broadcast_to(index & (LANES - 1), (8, LANES)), jnp.broadcast_to(index >> 7, (8, LANES))

    def take(tile, low):
        return jnp.take_along_axis(tile, low, axis=1, mode="promise_in_bounds")

    def gather_all(step):
        def whole(g, c):
            low, high = ghost_index(g)
            found = zeros8
            for t in range(TILES):
                found = jnp.where(high == t, take(own[8 * t : 8 * t + 8, :], low), found)
            ghost_out[g] = found
            return c

        def pair(g, c):
            both = []
            for u in range(2):
                low, high = ghost_index(2 * g + u)
                high = high - (sub >> 2)
                found = zeros8
                for t in range(TILES // 2):
                    found = jnp.where(high == 2 * t, take(paired[t], low), found)
                both.append(found + pltpu.roll(found, 4, 0))
            ghost_out_late[g] = jnp.where(sub < 4, both[0], both[1])
            return c

        if step == 0:
            lax.fori_loop(0, GHOST_TILES, whole, 0)
        else:
            for t in range(TILES // 2):
                first, second = own[16 * t : 16 * t + 8, :], own[16 * t + 8 : 16 * t + 16, :]
                paired[t] = jnp.where(sub < 4, first, pltpu.roll(second, 4, 0))
            lax.fori_loop(0, GHOST_TILES // 2, pair, 0)

    def send_ghosts(step):
        for j in range(6):

            @pl.when(slots[j][3])
            def _():
                ghost_copy(step, j).start()

    velocity = None
    for step in range(2):

        coords = [dense(k) for k in range(3)]
        centred = [coords[0], coords[1], coords[2] + ((gz.astype(f32) + 0.5) * side - 0.5)]
        powers = monomials(centred)
        for m, triple in enumerate(TRIPLES):
            for k in range(3):
                term = dense_strength[k]
                if powers[triple] is not None:
                    term = term * powers[triple]
                folded = functools.reduce(lambda a, b: a + b, [term[8 * i : 8 * i + 8] for i in range(TILES // 8)])
                partial[8 * (4 * m + k) : 8 * (4 * m + k) + 8, :] = folded
            if step == 0:
                partial[8 * (4 * m + 3) : 8 * (4 * m + 3) + 8, :] = zeros8
        summed = None
        for i in range(8):
            rows = partial[pl.ds(i, 4 * COUNT, stride=8), :]
            summed = rows if summed is None else summed + rows
        summed = jnp.concatenate([summed, jnp.zeros((MESSAGE - 4 * COUNT, LANES), f32)], axis=0)
        ones = jnp.ones((8, 3 * LANES), bf16)
        parts = jnp.concatenate([p.astype(bf16) for p in split3(summed)], axis=1)
        part = lax.dot_general(ones, parts, (((1,), (1,)), ((), ())), preferred_element_type=f32)[0:1]
        message[step, 0] = part

        if step == 0:
            gather_all(step)
            pl.semaphore_wait(barrier, len(partners))
        for d in range(1, deep):
            column_copy(step, d).start()
        if step == 1:
            gather_all(step)
        send_ghosts(step)

        def own_quads(i, c):
            for v in range(4):
                own_quad(4 * i + v)
            return c

        def own_quad(q):
            tiles = []
            for u in range(4):
                t = 4 * q + u
                raw = own[pl.ds(pl.multiple_of(8 * t, 8), 8), :]
                tiles.append(raw)
                rows = jnp.concatenate(target_rows(raw), axis=0).astype(bf16)
                for quarter in range(4):
                    target_feat[4 * t + quarter, 32 * quarter : 32 * quarter + 32, :] = rows
                if step == 0:
                    source_str[t] = strength_rows(raw)
            source_quad(q, tiles)

        if step == 0:
            target_feat[...] = jnp.zeros_like(target_feat)
        lax.fori_loop(0, TILES // 16, own_quads, 0)

        if step == 0:
            separation = (
                away_x.astype(f32),
                away_y.astype(f32),
                jnp.full((4, plane), (gz.astype(f32) + 0.5) * side - 0.5, f32),
            )
            for q, value in enumerate(derivatives(separation).values()):
                far_weights[4 * q : 4 * q + 4, :] = value

        else:
            for k in range(3):
                place(placer_start, start_flat, k, coords[k] + centre[k])
            for b in range(tall):
                for a in range(wide):
                    start_out[b, a] = start_flat[8 * (wide * b + a) : 8 * (wide * b + a) + 8, :]
            for d in range(1, tall):
                start_y_copy(d).start()
            for a in range(wide):
                start_mid[a, gy] = start_out[gy, a]

        all_column(step).wait_recv()
        total = message[step, 0]
        for d in range(1, deep):
            total = total + column_in[step, d - 1]
        message[step, 1] = total
        plane_in[step, rank] = total

        for d in others:
            plane_copy(step, d).start()

        for j in range(6):

            @pl.when(slots[j][2])
            def _():
                ghost_copy(step, j).wait_recv()

            axis, offset = slots[j][0], slots[j][1]
            moved = jnp.where(sub == axis, offset, 0.0)

            for q in range(GHOST_TILES // 4):
                tiles = []
                for u in range(4):
                    g = 4 * q + u
                    if step == 0:
                        raw = ghost_in[j, g]
                        source_str[TILES + j * GHOST_TILES + g] = strength_rows(raw)
                    elif u % 2 == 0:
                        raw = ghost_in_late[j, g // 2]
                    else:
                        raw = pltpu.roll(ghost_in_late[j, g // 2], 4, 0)
                    tiles.append(raw + moved)
                source_quad(TILES // 4 + j * (GHOST_TILES // 4) + q, tiles)

        def near(b, c):
            values = []
            for u in range(UNROLL):
                p = b * UNROLL + u
                t, s = targets[p], sources[p]
                gap = jnp.dot(source_feat[s >> 2], target_feat[4 * t + (s & 3)], preferred_element_type=f32)
                values.append(halves(lax.rsqrt(jnp.maximum(gap, core_sq))))
            for u in range(UNROLL):
                p = b * UNROLL + u
                pushed = source_str[sources[p]]
                pushed = jnp.concatenate([pushed, pushed], axis=1)
                both = jnp.concatenate(values[u], axis=0)
                contrib[pl.ds(pl.multiple_of(16 * p, 16), 16), :] = jnp.dot(
                    pushed, both, preferred_element_type=f32
                )
            return c

        lax.fori_loop(0, NPAIR // UNROLL // 2, near, 0)
        if step == 1:
            all_start_y().wait_recv()
            for d in range(1, wide):
                start_x_copy(d).start()
            start_in[gx] = start_mid[gx]
        lax.fori_loop(NPAIR // UNROLL // 2, NPAIR // UNROLL, near, 0)
        velocity = []
        for k in range(3):
            rows = contrib[pl.ds(3 + k, NPAIR, stride=16), :] + contrib[pl.ds(11 + k, NPAIR, stride=16), :]
            both = jnp.concatenate(halves(rows), axis=0)
            velocity.append(jnp.dot(chosen, both, preferred_element_type=f32))

        all_plane(step).wait_recv()
        for s in range(plane):
            gathered[s : s + 1, :] = plane_in[step, s]
        turned[...] = jnp.transpose(gathered[...])
        expansion = {}
        for m, inner in enumerate(TRIPLES):
            factor = (-1.0) ** sum(inner) / factorial(inner)
            source = jnp.where(is_far, turned[4 * m : 4 * m + 4, :] * factor, 0.0)
            for outer in TRIPLES:
                if sum(outer) + sum(inner) <= ORDER:
                    q = PLACE[tuple(a + b for a, b in zip(outer, inner))]
                    term = far_weights[4 * q : 4 * q + 4, :] * source
                    expansion[outer] = term if outer not in expansion else expansion[outer] + term
        for n, outer in enumerate(TRIPLES):
            value = jnp.sum(expansion[outer], axis=1, keepdims=True) * (1.0 / factorial(outer))
            local[4 * n : 4 * n + 4, :] = jnp.broadcast_to(value, (4, LANES))
        powers = monomials(coords)
        for n, outer in enumerate(TRIPLES):
            for k in range(3):
                term = jnp.broadcast_to(local[4 * n + k : 4 * n + k + 1, :], (TILES, LANES))
                if powers[outer] is not None:
                    term = term * powers[outer]
                velocity[k] = velocity[k] + term

        if step == 0:
            for k in range(3):
                own[pl.ds(k, TILES, stride=8), :] = coords[k] + time_step * velocity[k]

    for k in range(3):
        place(placer_speed, speed_out, k, velocity[k])

    for d in others:
        speed_copy(d).start()
    speed_in[speed_rows(rank), :] = speed_out[speed_rows(rank), :]
    all_start_x().wait_recv()
    for a in range(wide):
        for b in range(tall):
            start_flat[8 * (tall * a + b) : 8 * (tall * a + b) + 8, :] = start_in[a, b]
    for step in range(2):
        for j in range(6):

            @pl.when(slots[j][3])
            def _():
                ghost_copy(step, j).wait_send()

        all_column(step).wait_send()
        all_plane(step).wait_send()
    all_start_y().wait_send()
    all_start_x().wait_send()
    all_speed().wait_recv()
    for k in range(3):
        for r in range(CAP):
            held = pl.ds(3 * r + k, plane, stride=8)
            slot = pl.ds(r, plane, stride=CAP)
            out_vel[k, slot, :] = speed_in[held, :]
            out_pos[k, slot, :] = start_flat[held, :] + time_step * speed_in[held, :]
    all_speed().wait_send()


def hand_on(pos_in, vel_in, pos_out, vel_out, done):
    first = pltpu.make_async_copy(pos_in, pos_out, done.at[0])
    second = pltpu.make_async_copy(vel_in, vel_out, done.at[1])
    first.start()
    second.start()
    first.wait()
    second.wait()


def finish(positions, velocity):
    hbm = pl.BlockSpec(memory_space=pltpu.HBM)
    vmem = pl.BlockSpec(memory_space=pltpu.VMEM)
    positions, velocity = pl.pallas_call(
        hand_on,
        out_shape=tuple(jax.ShapeDtypeStruct(a.shape, a.dtype) for a in (positions, velocity)),
        in_specs=[vmem, vmem],
        out_specs=(hbm, hbm),
        scratch_shapes=[pltpu.SemaphoreType.DMA((2,))],
        name="hand_on",
    )(positions, velocity)
    return positions.transpose(1, 0, 2), velocity.transpose(1, 0, 2)


def per_device(offsets, strength, ghost_list, pair_targets, pair_sources, owners):
    sizes = tuple(lax.axis_size(axis) for axis in ("gx", "gy", "gz"))
    wide, tall, deep = sizes
    plane = wide * tall
    vmem = pl.BlockSpec(memory_space=pltpu.VMEM)
    smem = pl.BlockSpec(memory_space=pltpu.SMEM)
    hbm = pl.BlockSpec(memory_space=pltpu.HBM)
    shape = jax.ShapeDtypeStruct((3, plane * CAP, LANES), f32)
    dma = pltpu.SemaphoreType.DMA
    positions, velocity = pl.pallas_call(
        functools.partial(kernel, sizes),
        out_shape=(shape, shape),
        in_specs=[hbm, hbm, vmem, smem, vmem, smem, vmem],
        out_specs=(vmem, vmem),
        scratch_shapes=[
            pltpu.VMEM((3, SEG), f32),
            pltpu.VMEM((3, SEG), f32),
            pltpu.SemaphoreType.DMA((2,)),
            pltpu.VMEM((8 * TILES, LANES), f32),
            pltpu.VMEM((TILES // 2, 8, LANES), f32),
            pltpu.VMEM((GHOST_TILES, 8, LANES), f32),
            pltpu.VMEM((6, GHOST_TILES, 8, LANES), f32),
            pltpu.VMEM((GHOST_TILES // 2, 8, LANES), f32),
            pltpu.VMEM((6, GHOST_TILES // 2, 8, LANES), f32),
            pltpu.VMEM((4 * TILES, LANES, LANES), bf16),
            pltpu.VMEM((SOURCES // 4, LANES, LANES), bf16),
            pltpu.VMEM((SOURCES, 16, LANES), bf16),
            pltpu.VMEM((NPAIR * 16, LANES), f32),
            pltpu.VMEM((4 * COUNT * 8, LANES), f32),
            pltpu.VMEM((2, 2, 1, MESSAGE), f32),
            pltpu.VMEM((2, deep - 1, 1, MESSAGE), f32),
            pltpu.VMEM((2, plane, 1, MESSAGE), f32),
            pltpu.VMEM((plane, MESSAGE), f32),
            pltpu.VMEM((MESSAGE, plane), f32),
            pltpu.VMEM((4 * COUNT, LANES), f32),
            pltpu.VMEM((4 * COUNT, plane), f32),
            pltpu.VMEM((plane * 8, LANES), f32),
            pltpu.VMEM((tall, wide, 8, LANES), f32),
            pltpu.VMEM((wide, tall, 8, LANES), f32),
            pltpu.VMEM((wide, tall, 8, LANES), f32),
            pltpu.VMEM((plane * 8, LANES), f32),
            pltpu.VMEM((plane * 8, LANES), f32),
            dma((2, 6)),
            dma((2, 6)),
            dma((2,)),
            dma((2,)),
            dma((2,)),
            dma((2,)),
            dma((3,)),
            dma((3,)),
        ],
        compiler_params=pltpu.CompilerParams(
            collective_id=0, has_side_effects=True, vmem_limit_bytes=62 << 20
        ),
        name="dislocation_steps",
    )(offsets, strength, ghost_list, pair_targets, pair_targets, pair_sources, owners.reshape(1, TILES))
    return finish(positions, velocity)


def solution(mesh):
    return jax.shard_map(
        per_device,
        mesh=mesh,
        in_specs=(
            P(None, ("gx", "gy", "gz")),
            P(None, ("gx", "gy", "gz")),
            P(("gx", "gy", "gz")),
            P(("gx", "gy", "gz")),
            P(("gx", "gy", "gz")),
            P(("gx", "gy", "gz"), None),
        ),
        out_specs=(P(("gx", "gy", "gz"), None, None), P(("gx", "gy", "gz"), None, None)),
        check_vma=False,
    )
```
